32 devices in a mesh: groups: 2 (over y), row: 4 (over z), col: 4 (over x, core).
Axes of the slice: x: 2, y: 2, z: 4, core: 2. Of those that a mesh axis runs over, the one named last changes fastest.
Arguments:
- grad_x: bfloat16 [3, 3072, 1536], P(None, ('groups', 'row'), 'col'), parts along dimension 1, may hold values from -4 to 4
- grad_y: bfloat16 [3, 3072, 1536], P(None, ('groups', 'row'), 'col'), parts along dimension 1, may hold values from -4 to 4
- seam_mask: int32 [3072, 1536], P(('groups', 'row'), 'col'), parts along dimension 0, may hold values 0 or 1
- tile_offset: int32 [3, 8, 4], P(None, 'groups'), parts along dimension 1, may hold values from -8 to 8
Outputs:
- stitched: float32 [3, 3072, 1536], P(None, ('groups', 'row'), 'col'), parts along dimension 1
The draws below stay inside these ranges and needn't reach their ends.
There are 2 independent parts, one for each index of `groups`. The reference program is written for one: setup_inputs(seed, part) draws one part's arguments, and reference() takes and returns one part's arrays. A program takes and returns all parts, laid end to end along the dimension named above; each array names one. Nothing has to cross between parts.
Inputs may be any that keep to these rules, and one draw needn't show every extreme that they name: `tile_offset`: whole quarter steps of exposure.
All inputs are finite; a program needn't handle non-finite values. No bound on the sum of `seam_mask` on one device may be relied on, other than what follows from the above.
Results may differ from the reference program's by a relative error of at most 0.0045.
Values sent between devices are 32-bit elements; how exact they have to be, the bound alone decides.
A program may use at most 64 MiB of HBM per device.

```python
import math
import jax
import jax.numpy as jnp
from jax import lax

TH = 384
TW = 384
CH = 3
M = 128
SWEEPS = 8
NX = 1536
NY = 1536
N_ROW = 4
N_COL = 4


def place_ends(result, stream_key, low, top_value):
    spot = [jax.random.randint(jax.random.fold_in(stream_key, axis), (), 0, length) for axis, length in enumerate(result.shape)]
    longest = result.shape.index(max(result.shape))
    beside = spot[:longest] + [(spot[longest] + 1) % result.shape[longest]] + spot[longest + 1:]
    return result.at[tuple(spot)].set(low).at[tuple(beside)].set(top_value)


def shard_levels(rng, extent, split, low, top_value):
    loudness, own = 1.0, jax.random.fold_in(rng, 6)
    for dim, parts in split:
        heights = jnp.exp(jax.random.uniform(jax.random.fold_in(own, dim), (parts,), jnp.float32, low / len(split), top_value / len(split)))
        loudness = loudness * jnp.repeat(heights, extent[dim] // parts).reshape([-1 if axis == dim else 1 for axis in range(len(extent))])
    return loudness


def normal_values(stream_key, extent, scale, most, cuts=(), held_as=jnp.bfloat16):
    result = scale * jax.random.normal(stream_key, extent, jnp.float32)
    if cuts:
        result = result * shard_levels(stream_key, extent, cuts, -0.22, 0.18)
    return jnp.clip(result, -most, most).astype(held_as)


def setup_inputs(seed: int = 0, part: int = 0) -> dict:
    seeds = jax.random.split(jax.random.key(seed), 5)
    part_splits = jax.random.split(jax.random.fold_in(seeds[4], part), 5)
    return {
        "grad_x": normal_values(part_splits[0], (CH, NX, NY), 0.5, 4.0, ((1, 4), (2, 4))),
        "grad_y": normal_values(part_splits[1], (CH, NX, NY), 0.5, 4.0, ((1, 4), (2, 4))),
        "seam_mask": place_ends((jax.random.randint(part_splits[2], (NX, NY), 0, 4) < 1).astype(jnp.int32), jax.random.fold_in(part_splits[2], 1), 0, 1),
        "tile_offset": place_ends(jax.random.randint(part_splits[3], (CH, N_ROW, N_COL), -8, 9), jax.random.fold_in(part_splits[3], 1), -8, 8).astype(jnp.int32),
    }


def cosine_table(count, modes, start, length):
    order = jnp.arange(modes, dtype=jnp.int32)
    places = start + jnp.arange(length, dtype=jnp.int32)
    phases = order[:, None] * (2 * places[None, :] + 1) % (4 * count)
    angles = math.pi / (2 * count) * phases.astype(jnp.float32)
    scales = jnp.where(order == 0, math.sqrt(1.0 / count), math.sqrt(2.0 / count)).astype(jnp.float32)
    return scales[:, None] * jnp.cos(angles)

def eigen_line(count, start, length):
    order = (start + jnp.arange(length, dtype=jnp.int32)).astype(jnp.float32)
    return 2.0 - 2.0 * jnp.cos(math.pi / count * order)

def neighbour_sum(padded):
    return padded[:, :-2, 1:-1] + padded[:, 2:, 1:-1] + padded[:, 1:-1, :-2] + padded[:, 1:-1, 2:]

def reference(grad_x, grad_y, seam_mask, tile_offset):
    damping = 1.0 - 0.75 * seam_mask.astype(jnp.float32)
    edge_x = grad_x.astype(jnp.float32) * damping
    edge_y = grad_y.astype(jnp.float32) * damping
    levels = 0.25 * tile_offset.astype(jnp.float32)
    rows_all = jnp.arange(NX, dtype=jnp.int32)
    cols_all = jnp.arange(NY, dtype=jnp.int32)
    tile_row = rows_all // TH
    tile_col = cols_all // TW
    next_row = jnp.minimum(tile_row + 1, N_ROW - 1)
    next_col = jnp.minimum(tile_col + 1, N_COL - 1)
    here = levels[:, tile_row][:, :, tile_col]
    step_x = levels[:, next_row][:, :, tile_col] - here
    step_y = levels[:, tile_row][:, :, next_col] - here
    last_row = (rows_all % TH == TH - 1).astype(jnp.float32)[:, None]
    last_col = (cols_all % TW == TW - 1).astype(jnp.float32)[None, :]
    edge_x = (edge_x + last_row * step_x) * (rows_all < NX - 1).astype(jnp.float32)[:, None]
    edge_y = (edge_y + last_col * step_y) * (cols_all < NY - 1).astype(jnp.float32)[None, :]
    before_x = jnp.pad(edge_x[:, :-1, :], ((0, 0), (1, 0), (0, 0)))
    before_y = jnp.pad(edge_y[:, :, :-1], ((0, 0), (0, 0), (1, 0)))
    source = -(edge_x - before_x + (edge_y - before_y))
    screen = 0.5 * math.pi * math.pi / (NX * NY)
    table_x = cosine_table(NX, M, 0, NX)
    table_y = cosine_table(NY, M, 0, NY)
    highest = lax.Precision.HIGHEST
    halves = jnp.einsum('cij,lj->cil', source, table_y, precision=highest)
    spectral = jnp.einsum('ki,cil->ckl', table_x, halves, precision=highest)
    eigen_sum = screen + eigen_line(NX, 0, M)[:, None] + eigen_line(NY, 0, M)[None, :]
    coeffs = spectral / eigen_sum
    backed = jnp.einsum('ckl,lj->ckj', coeffs, table_y, precision=highest)
    stitched = jnp.einsum('ki,ckj->cij', table_x, backed, precision=highest)
    counts = ((rows_all > 0).astype(jnp.float32) + (rows_all < NX - 1).astype(jnp.float32))[:, None]
    counts = counts + ((cols_all > 0).astype(jnp.float32) + (cols_all < NY - 1).astype(jnp.float32))[None, :]
    denominator = screen + counts
    for sweep_index in range(SWEEPS):
        padded = jnp.pad(stitched, ((0, 0), (1, 1), (1, 1)))
        stitched = (source + neighbour_sum(padded)) / denominator
    return stitched
```

```python
import functools
import math

import jax
import jax.numpy as jnp
import ml_dtypes
import numpy as np
from jax import lax
from jax.experimental import pallas as pl
from jax.experimental.pallas import tpu as pltpu
from jax.sharding import PartitionSpec as P

M = 128
SWEEPS = 8
LANES = 128
PAD = 16
MESH = pl.DeviceIdType.MESH
F32 = jnp.float32
BF16 = jnp.bfloat16


def np_split(x):
    hi = x.astype(np.float32).astype(ml_dtypes.bfloat16)
    lo = (x - hi.astype(np.float64)).astype(np.float32).astype(ml_dtypes.bfloat16)
    return hi, lo


def np_tables(count):
    k = np.arange(M)
    i = np.arange(count)
    scale = np.where(k == 0, math.sqrt(1.0 / count), math.sqrt(2.0 / count))
    cos = scale * np.cos(np.pi / (2 * count) * ((k * (2 * i[:, None] + 1)) % (4 * count)))
    sin = (
        -2.0
        * scale
        * np.sin(np.pi * k / (2 * count))
        * np.sin(np.pi / count * ((k * (i[:, None] + 1)) % (2 * count)))
    )
    eigen = 2.0 - 2.0 * np.cos(np.pi * k / count)
    return cos, sin, eigen


def split(x):
    hi = x.astype(BF16)
    return hi, (x - hi.astype(F32)).astype(BF16)


def iota(shape, dim):
    return lax.broadcasted_iota(jnp.int32, shape, dim)


def first_kernel(
    dims,
    gx_ref, gy_ref, mask_ref, off_ref, ty_hbm, tx_hbm,
    ts_ref, sp_ref,
    E, S, XA, XB, inv, ty, tx, part, pack, cols, r1, acc, r2, fin, acc2,
    tab_sem, cs_send, cs_recv, rs_send, rs_recv,
    p1s, p1r, p2s, p2r, p3s, p3r, p4s, p4r,
):
    R, C, CH, TH, TW, screen = dims
    W = TW + LANES
    half = TH // 2
    group = lax.axis_index("groups")
    row = lax.axis_index("row")
    col = lax.axis_index("col")
    modes = CH * M
    crows = modes // C
    nparts = min(R, crows // 8)
    prow = crows // nparts

    def at(r, c):
        return (group, r, c)

    ty_copy = pltpu.make_async_copy(ty_hbm.at[pl.ds(col * TW, TW)], ty, tab_sem.at[0])
    tx_copy = pltpu.make_async_copy(tx_hbm.at[row], tx, tab_sem.at[1])
    ty_copy.start()
    tx_copy.start()

    cols[...] = jnp.zeros_like(cols)
    E[:, 0:PAD, :] = jnp.zeros((2 * CH, PAD, W), F32)
    E[:, PAD + TH :, :] = jnp.zeros((2 * CH, PAD, W), F32)

    barrier = pltpu.get_barrier_semaphore()
    for off in range(1, C):
        pl.semaphore_signal(
            barrier, inc=1, device_id=at(row, lax.rem(col + off, C)), device_id_type=MESH
        )
    for off in range(1, R):
        pl.semaphore_signal(
            barrier, inc=1, device_id=at(lax.rem(row + off, R), col), device_id_type=MESH
        )

    here = 0.25 * off_ref[0 * R * C + row * C + col].astype(F32)
    below_row = jnp.minimum(row + 1, R - 1)
    right_col = jnp.minimum(col + 1, C - 1)
    stepx, stepy = [], []
    for c in range(CH):
        here = 0.25 * off_ref[c * R * C + row * C + col].astype(F32)
        stepx.append(0.25 * off_ref[c * R * C + below_row * C + col].astype(F32) - here)
        stepy.append(0.25 * off_ref[c * R * C + row * C + right_col].astype(F32) - here)
    ER = 32

    def edge_rows(t, carry):
        r0 = pl.multiple_of(t * ER, ER)
        rows = iota((ER, 1), 0) + r0
        lanes = iota((1, TW), 1)
        damp = 1.0 - 0.75 * mask_ref[pl.ds(r0, ER), :].astype(F32)
        last_row = (rows == TH - 1).astype(F32)
        last_col = (lanes == TW - 1).astype(F32)
        keep_row = jnp.where((rows == TH - 1) & (row == R - 1), 0.0, 1.0)
        keep_col = jnp.where((lanes == TW - 1) & (col == C - 1), 0.0, 1.0)
        b0 = pl.multiple_of(r0 + PAD, 8)
        for c in range(CH):
            ex = (gx_ref[c, pl.ds(r0, ER), :].astype(F32) * damp + last_row * stepx[c]) * keep_row
            ey = (gy_ref[c, pl.ds(r0, ER), :].astype(F32) * damp + last_col * stepy[c]) * keep_col
            E[c, pl.ds(b0, ER), 0:TW] = ex
            E[CH + c, pl.ds(b0, ER), 0:TW] = ey
        return carry

    lax.fori_loop(0, TH // ER, edge_rows, 0)

    lane = iota((half, LANES), 1)
    for side in range(2):
        total = jnp.zeros((half, LANES), F32)
        for h in range(2):
            for a in range(2 * CH):
                rows = slice(PAD + h * half, PAD + (h + 1) * half)
                tile = slice(TW - LANES, TW) if side == 0 else slice(0, LANES)
                spot = 8 * a + 64 * h
                shift = (spot + (8 if side == 0 else 0)) % LANES
                x = E[a, rows, tile]
                if shift:
                    x = pltpu.roll(x, shift, 1)
                total = jnp.where((lane >= spot) & (lane < spot + 8), x, total)
        pack[side] = total

    pl.semaphore_wait(barrier, C - 1 + R - 1)
    to_right = pltpu.make_async_remote_copy(
        src_ref=pack.at[0], dst_ref=cols.at[0], send_sem=cs_send.at[0], recv_sem=cs_recv.at[0],
        device_id=at(row, jnp.minimum(col + 1, C - 1)), device_id_type=MESH,
    )
    to_left = pltpu.make_async_remote_copy(
        src_ref=pack.at[1], dst_ref=cols.at[1], send_sem=cs_send.at[1], recv_sem=cs_recv.at[1],
        device_id=at(row, jnp.maximum(col - 1, 0)), device_id_type=MESH,
    )
    pl.when(col < C - 1)(to_right.start)
    pl.when(col > 0)(to_left.start)

    IR = 32
    def inv_rows(t, carry):
        r0 = pl.multiple_of(t * IR, IR)
        places = iota((IR, 1), 0) + r0 - PAD + row * TH
        lanes = iota((1, W), 1)
        lanes = jnp.where(lanes < TW + 8, lanes, lanes - W) + col * TW
        crow = (places > 0).astype(F32) + (places < R * TH - 1).astype(F32)
        ccol = (lanes > 0).astype(F32) + (lanes < C * TW - 1).astype(F32)
        inside = ((places >= 0) & (places < R * TH)).astype(F32) * (
            (lanes >= 0) & (lanes < C * TW)
        ).astype(F32)
        inv[pl.ds(r0, IR), :] = inside / (screen + crow + ccol)
        return carry

    lax.fori_loop(0, (TH + 2 * PAD) // IR, inv_rows, 0)

    ty_copy.wait()
    tx_copy.wait()
    for c in range(CH):
        hs = []
        for d in range(2):
            e = E[d * CH + c, PAD : PAD + TH, 0:TW].astype(BF16)
            h = jnp.dot(e, ty[:, d * 2 * M : (d + 1) * 2 * M], preferred_element_type=F32)
            hs.append(h[:, :M] + h[:, M:])
        h = jnp.concatenate(hs, axis=0)
        hi, lo = split(h)
        o = jnp.dot(tx[...], jnp.concatenate([hi, lo], axis=1), preferred_element_type=F32)
        part[c * M : (c + 1) * M, :] = (o[:M, :M] + o[M:, :M]) + (o[:M, M:] + o[M:, M:])

    p1 = []
    for off in range(1, C):
        d = lax.rem(col + off, C)
        cp = pltpu.make_async_remote_copy(
            src_ref=part.at[pl.ds(pl.multiple_of(d * crows, 8), crows)], dst_ref=r1.at[off],
            send_sem=p1s.at[off], recv_sem=p1r.at[off],
            device_id=at(row, d), device_id_type=MESH,
        )
        cp.start()
        p1.append(cp)

    pl.when(col > 0)(to_right.wait_recv)
    pl.when(col < C - 1)(to_left.wait_recv)
    for a in range(2 * CH):
        for h in range(2):
            rows = slice(PAD + h * half, PAD + (h + 1) * half)
            spot = 8 * a + 64 * h
            left = pltpu.roll(cols[0], (120 - spot) % LANES, 1)
            right = cols[1]
            if spot:
                right = pltpu.roll(right, LANES - spot, 1)
            E[a, rows, TW:W] = jnp.where(lane < 8, right, jnp.where(lane >= 120, left, 0.0))
    to_below = pltpu.make_async_remote_copy(
        src_ref=E.at[:, pl.ds(PAD + TH - 8, 8), :], dst_ref=E.at[:, pl.ds(PAD - 8, 8), :],
        send_sem=rs_send.at[0], recv_sem=rs_recv.at[0],
        device_id=at(jnp.minimum(row + 1, R - 1), col), device_id_type=MESH,
    )
    to_above = pltpu.make_async_remote_copy(
        src_ref=E.at[:, pl.ds(PAD, 8), :], dst_ref=E.at[:, pl.ds(PAD + TH, 8), :],
        send_sem=rs_send.at[1], recv_sem=rs_recv.at[1],
        device_id=at(jnp.maximum(row - 1, 0), col), device_id_type=MESH,
    )
    pl.when(row < R - 1)(to_below.start)
    pl.when(row > 0)(to_above.start)

    for cp in p1:
        cp.wait_recv()
    total = part[pl.ds(pl.multiple_of(col * crows, 8), crows), :]
    for off in range(1, C):
        total = total + r1[off]
    acc[...] = total

    def guarded(cond, f):
        if nparts == R:
            f()
        else:
            pl.when(cond)(f)

    p2 = []
    for off in range(1, R):
        d = lax.rem(row + off, R)
        dd = jnp.minimum(d, nparts - 1) if nparts < R else d
        cp = pltpu.make_async_remote_copy(
            src_ref=acc.at[pl.ds(pl.multiple_of(dd * prow, 8), prow)], dst_ref=r2.at[off],
            send_sem=p2s.at[off], recv_sem=p2r.at[off],
            device_id=at(d, col), device_id_type=MESH,
        )
        guarded(d < nparts, cp.start)
        p2.append((cp, d))

    pl.when(row > 0)(to_below.wait_recv)
    pl.when(row < R - 1)(to_above.wait_recv)
    HR = 40
    nchunk = (TH + 16) // HR

    XA[:, 0:8, :] = jnp.zeros((CH, 8, W), F32)
    XA[:, PAD + TH + 8 :, :] = jnp.zeros((CH, 8, W), F32)
    XB[:, 0:8, :] = jnp.zeros((CH, 8, W), F32)
    XB[:, PAD + TH + 8 :, :] = jnp.zeros((CH, 8, W), F32)

    def source_rows(t, carry):
        b0 = pl.multiple_of(8 + t * HR, 8)
        d = inv[pl.ds(b0, HR), :]
        for c in range(CH):
            wide = E[c, pl.ds(pl.multiple_of(b0 - 8, 8), HR + 8), :]
            ey = E[CH + c, pl.ds(b0, HR), :]
            s = (wide[7 : 7 + HR] - wide[8:]) + (pltpu.roll(ey, 1, 1) - ey)
            s = s * d
            S[c, pl.ds(b0, HR), :] = s
            XA[c, pl.ds(b0, HR), :] = s
        return carry

    lax.fori_loop(0, nchunk, source_rows, 0)

    def sweep(src, dst):
        def rows(t, carry):
            b0 = pl.multiple_of(8 + t * HR, 8)
            d = inv[pl.ds(b0, HR), :]
            for c in range(CH):
                wide = src[c, pl.ds(pl.multiple_of(b0 - 8, 8), HR + 16), :]
                mid = wide[8 : 8 + HR]
                nb = (wide[7 : 7 + HR] + wide[9 : 9 + HR]) + (
                    pltpu.roll(mid, 1, 1) + pltpu.roll(mid, W - 1, 1)
                )
                dst[c, pl.ds(b0, HR), :] = S[c, pl.ds(b0, HR), :] + nb * d
            return carry

        lax.fori_loop(0, nchunk, rows, 0)

    sweep(XA, XB)
    sweep(XB, XA)

    for cp, d in p2:
        guarded(row < nparts, cp.wait_recv)
    me = jnp.minimum(row, nparts - 1) if nparts < R else row
    mine = pl.ds(pl.multiple_of(me * prow, 8), prow)

    def sum_rows():
        total = acc[mine, :]
        for off in range(1, R):
            total = total + r2[off]
        fin[...] = total
        acc2[mine, :] = total

    guarded(row < nparts, sum_rows)
    p3 = []
    for off in range(1, R):
        d = lax.rem(row + off, R)
        s = lax.rem(row + R - off, R)
        cp = pltpu.make_async_remote_copy(
            src_ref=fin, dst_ref=acc2.at[mine],
            send_sem=p3s.at[off], recv_sem=p3r.at[off],
            device_id=at(d, col), device_id_type=MESH,
        )
        guarded(row < nparts, cp.start)
        p3.append((cp, s))

    sweep(XA, XB)
    sweep(XB, XA)

    for cp, s in p3:
        guarded(s < nparts, cp.wait_recv)
    own = pl.ds(pl.multiple_of(col * crows, 8), crows)
    p4 = []
    for off in range(1, C):
        d = lax.rem(col + off, C)
        cp = pltpu.make_async_remote_copy(
            src_ref=acc2, dst_ref=sp_ref.at[own],
            send_sem=p4s.at[off], recv_sem=p4r.at[off],
            device_id=at(row, d), device_id_type=MESH,
        )
        cp.start()
        p4.append(cp)
    sp_ref[own, :] = acc2[...]

    sweep(XA, XB)
    sweep(XB, XA)
    LR = 32

    def last_rows(t, carry):
        b0 = pl.multiple_of(PAD + t * LR, 8)
        o0 = pl.multiple_of(t * LR, 8)
        d = inv[pl.ds(b0, LR), 0:TW]
        for c in range(CH):
            wide = XA[c, pl.ds(pl.multiple_of(b0 - 8, 8), LR + 16), :]
            mid = wide[8 : 8 + LR]
            side = pltpu.roll(mid, 1, 1) + pltpu.roll(mid, W - 1, 1)
            nb = (wide[7 : 7 + LR] + wide[9 : 9 + LR])[:, 0:TW] + side[:, 0:TW]
            ts_ref[c, pl.ds(o0, LR), :] = S[c, pl.ds(b0, LR), 0:TW] + nb * d
        return carry

    lax.fori_loop(0, TH // LR, last_rows, 0)

    for cp in p4:
        cp.wait_recv()
    pl.when(col < C - 1)(to_right.wait_send)
    pl.when(col > 0)(to_left.wait_send)
    pl.when(row < R - 1)(to_below.wait_send)
    pl.when(row > 0)(to_above.wait_send)
    for cp in p1:
        cp.wait_send()
    for cp, d in p2:
        guarded(d < nparts, cp.wait_send)
    for cp, d in p3:
        guarded(row < nparts, cp.wait_send)
    for cp in p4:
        cp.wait_send()


def last_kernel(
    dims,
    pos_ref, sp_ref, ts_ref, tb_ref, mu_ref, cxk_ref, cxr_ref, cyb_ref, cys_ref, cyk_ref,
    out_ref, H,
):
    R, C, CH, TH, TW, screen = dims
    W = TW + LANES
    highest = lax.Precision.HIGHEST
    row, col = pos_ref[0], pos_ref[1]
    top, bottom = row == 0, row == R - 1
    left, right = col == 0, col == C - 1
    sp = sp_ref[...]
    coeffs = sp * tb_ref[0]
    moved = sp * tb_ref[1]

    hi, lo = split(moved)
    both = jnp.concatenate([hi, lo], axis=1)
    h = jnp.dot(cxr_ref[...], jnp.concatenate([both, both], axis=0), preferred_element_type=F32)
    H[...] = h[:, :M] + h[:, M:]

    @pl.when(top | bottom)
    def _():
        strip = jnp.where(top, 1, 0)
        tab = cxk_ref[...]
        lanes = jnp.where(top, 0.0, 1.0)
        first, last = tab[:, 0:LANES], tab[:, TW - LANES : TW]
        pick = jnp.where(top, first, last)
        u = lax.dot_general(
            pick, coeffs, (((0,), (0,)), ((), ())), precision=highest, preferred_element_type=F32
        )
        u = jnp.where(top, u[0:16], u[LANES - 16 :])
        r = iota((16, M), 0)
        edge = (top & (r == 0)) | (bottom & (r == 15))
        scale = 1.0 / (screen + jnp.where(edge, 3.0, 4.0))
        own = 2.0 - mu_ref[...]
        for _ in range(SWEEPS):
            up = jnp.where(r == 0, 0.0, pltpu.roll(u, 1, 0))
            down = jnp.where(r == 15, 0.0, pltpu.roll(u, 15, 0))
            u = (up + down + own * u) * scale

        @pl.when(top)
        def _():
            H[0:8, :] = u[0:8]

        @pl.when(bottom)
        def _():
            H[TH - 8 : TH, :] = u[8:16]

    hh, hl = split(H[...])
    lhs = jnp.concatenate([hh, hl, hh], axis=1)
    out_ref[0] = jnp.dot(lhs, cyb_ref[...], preferred_element_type=F32) + ts_ref[0]

    @pl.when(left | right)
    def _():
        cy = jnp.where(left, cys_ref[0:16, :], cys_ref[TW - 16 : TW, :])
        z = lax.dot_general(
            cy, coeffs, (((1,), (1,)), ((), ())), precision=highest, preferred_element_type=F32
        )
        w = jnp.dot(z, cxk_ref[...], precision=highest, preferred_element_type=F32)
        r = iota((16, W), 0)
        lanes = iota((16, W), 1)
        place = jnp.where(lanes < TW + 8, lanes, lanes - W) + row * TH
        inside = (place >= 0) & (place < R * TH)
        cx = (place > 0).astype(F32) + (place < R * TH - 1).astype(F32)
        edge = (left & (r == 0)) | (right & (r == 15))
        scale = jnp.where(inside, 1.0, 0.0) / (screen + cx + jnp.where(edge, 1.0, 2.0))
        w = jnp.where(inside, w, 0.0)
        for _ in range(SWEEPS):
            up = jnp.where(r == 0, 0.0, pltpu.roll(w, 1, 0))
            down = jnp.where(r == 15, 0.0, pltpu.roll(w, 15, 0))
            w = (up + down + (pltpu.roll(w, 1, 1) + pltpu.roll(w, W - 1, 1))) * scale
        wide = jnp.concatenate(
            [w[:, 0:TW], jnp.zeros((LANES - 16, TW), F32)], axis=0
        )
        wt = wide.T
        lane = iota((TW, LANES), 1)

        @pl.when(left)
        def _():
            ts = ts_ref[0, :, 0:LANES]
            out_ref[0, :, 0:LANES] = jnp.where(lane < 8, wt + ts, out_ref[0, :, 0:LANES])

        @pl.when(right)
        def _():
            ts = ts_ref[0, :, TW - LANES : TW]
            turned = pltpu.roll(wt, LANES - 16, 1)
            out_ref[0, :, TW - LANES : TW] = jnp.where(
                lane >= LANES - 8, turned + ts, out_ref[0, :, TW - LANES : TW]
            )


def body(grad_x, grad_y, seam_mask, tile_offset, tables):
    CH, TH, TW = grad_x.shape
    R = lax.axis_size("row")
    C = lax.axis_size("col")
    NX, NY = TH * R, TW * C
    screen = 0.5 * math.pi * math.pi / (NX * NY)
    dims = (R, C, CH, TH, TW, screen)
    W = TW + LANES
    modes = CH * M
    crows = modes // C
    nparts = min(R, crows // 8)
    prow = crows // nparts
    ty, tx, tb, mu, cxk, cxr, cyb, cys, cyk = tables
    vmem = pl.BlockSpec(memory_space=pltpu.VMEM)
    smem = pl.BlockSpec(memory_space=pltpu.SMEM)
    anys = pl.BlockSpec(memory_space=pl.ANY)
    rows = TH + 2 * PAD
    dma = pltpu.SemaphoreType.DMA
    ts, sp = pl.pallas_call(
        functools.partial(first_kernel, dims),
        out_shape=(
            jax.ShapeDtypeStruct((CH, TH, TW), F32),
            jax.ShapeDtypeStruct((modes, M), F32),
        ),
        in_specs=[vmem, vmem, vmem, smem, anys, anys],
        out_specs=(vmem, vmem),
        scratch_shapes=[
            pltpu.VMEM((2 * CH, rows, W), F32),
            pltpu.VMEM((CH, rows, W), F32),
            pltpu.VMEM((CH, rows, W), F32),
            pltpu.VMEM((CH, rows, W), F32),
            pltpu.VMEM((rows, W), F32),
            pltpu.VMEM((TW, 4 * M), BF16),
            pltpu.VMEM((2 * M, 2 * TH), BF16),
            pltpu.VMEM((modes, M), F32),
            pltpu.VMEM((2, TH // 2, LANES), F32),
            pltpu.VMEM((2, TH // 2, LANES), F32),
            pltpu.VMEM((C, crows, M), F32),
            pltpu.VMEM((crows, M), F32),
            pltpu.VMEM((R, prow, M), F32),
            pltpu.VMEM((prow, M), F32),
            pltpu.VMEM((crows, M), F32),
            dma((2,)), dma((2,)), dma((2,)), dma((2,)), dma((2,)),
            dma((C,)), dma((C,)), dma((R,)), dma((R,)),
            dma((R,)), dma((R,)), dma((C,)), dma((C,)),
        ],
        compiler_params=pltpu.CompilerParams(
            collective_id=0, has_side_effects=True, vmem_limit_bytes=48 * 2**20
        ),
        name="sums_and_sweeps",
    )(grad_x, grad_y, seam_mask, tile_offset.reshape(-1), ty, tx)

    pos = jnp.stack([lax.axis_index("row"), lax.axis_index("col")]).astype(jnp.int32)
    here = lambda i, p: (p[0], 0)
    spec = pltpu.PrefetchScalarGridSpec(
        num_scalar_prefetch=1,
        grid=(CH,),
        in_specs=[
            pl.BlockSpec((M, M), lambda i, p: (i, 0)),
            pl.BlockSpec((1, TH, TW), lambda i, p: (i, 0, 0)),
            pl.BlockSpec((2, M, M), lambda i, p: (0, 0, 0)),
            pl.BlockSpec((1, M), lambda i, p: (0, 0)),
            pl.BlockSpec((M, W), lambda i, p: (p[0], 0)),
            pl.BlockSpec((TH, 2 * M), lambda i, p: (p[0], 0)),
            pl.BlockSpec((3 * M, TW), lambda i, p: (0, p[1])),
            pl.BlockSpec((TW, M), lambda i, p: (p[1], 0)),
            pl.BlockSpec((8, LANES), lambda i, p: (0, 0)),
        ],
        out_specs=pl.BlockSpec((1, TH, TW), lambda i, p: (i, 0, 0)),
        scratch_shapes=[pltpu.VMEM((TH, M), F32)],
    )
    return pl.pallas_call(
        functools.partial(last_kernel, dims),
        grid_spec=spec,
        out_shape=jax.ShapeDtypeStruct((CH, TH, TW), F32),
        compiler_params=pltpu.CompilerParams(vmem_limit_bytes=40 * 2**20),
        name="synthesis",
    )(pos, sp, ts, tb, mu, cxk, cxr, cyb, cys, cyk)


def solution(mesh):
    in_specs = (
        P(None, ("groups", "row"), "col"),
        P(None, ("groups", "row"), "col"),
        P(("groups", "row"), "col"),
        P(None, "groups", None),
        P(),
    )
    out_specs = P(None, ("groups", "row"), "col")
    R, C = mesh.shape["row"], mesh.shape["col"]
    G = mesh.shape["groups"]

    def whole(grad_x, grad_y, seam_mask, tile_offset):
        NX, NY = grad_x.shape[1] // G, grad_x.shape[2]
        TH, TW = NX // R, NY // C
        W = TH + LANES
        screen = 0.5 * math.pi * math.pi / (NX * NY)
        cx, sx, ex = np_tables(NX)
        cy, sy, ey = np_tables(NY)
        ty = np.concatenate(np_split(cy) + np_split(sy), axis=1)
        tiles = [
            np.concatenate([sx[r * TH : (r + 1) * TH].T, cx[r * TH : (r + 1) * TH].T], axis=1)
            for r in range(R)
        ]
        tx = np.stack([np.concatenate(np_split(t), axis=0) for t in tiles])
        lam = ex[:, None] + ey[None, :]
        tb = np.stack([1.0 / (screen + lam), ((4.0 - lam) / (4.0 + screen)) ** SWEEPS / (screen + lam)])
        cxk = np.zeros((R, M, W))
        for r in range(R):
            cxk[r, :, :TH] = cx[r * TH : (r + 1) * TH].T
            if r > 0:
                cxk[r, :, W - 8 :] = cx[r * TH - 8 : r * TH].T
            if r < R - 1:
                cxk[r, :, TH : TH + 8] = cx[(r + 1) * TH : (r + 1) * TH + 8].T
        cxr = np.concatenate(np_split(cx), axis=1)
        hi, lo = np_split(cy.T)
        cyb = np.concatenate([hi, hi, lo], axis=0)
        tables = (
            jnp.asarray(ty), jnp.asarray(tx),
            jnp.asarray(tb.astype(np.float32)),
            jnp.asarray(ey[None, :].astype(np.float32)),
            jnp.asarray(cxk.reshape(R * M, W).astype(np.float32)),
            jnp.asarray(cxr), jnp.asarray(cyb),
            jnp.asarray(cy.astype(np.float32)),
            jnp.zeros((8, LANES), F32),
        )
        f = jax.shard_map(body, mesh=mesh, in_specs=in_specs, out_specs=out_specs, check_vma=False)
        return f(grad_x, grad_y, seam_mask, tile_offset, tables)

    return whole
```

```python
import functools
import math

import jax
import jax.numpy as jnp
import ml_dtypes
import numpy as np
from jax import lax
from jax.experimental import pallas as pl
from jax.experimental.pallas import tpu as pltpu
from jax.sharding import PartitionSpec as P

M = 128
SWEEPS = 8
LANES = 128
PAD = 16
MESH = pl.DeviceIdType.MESH
F32 = jnp.float32
BF16 = jnp.bfloat16


def np_split(x):
    hi = x.astype(np.float32).astype(ml_dtypes.bfloat16)
    lo = (x - hi.astype(np.float64)).astype(np.float32).astype(ml_dtypes.bfloat16)
    return hi, lo


def np_tables(count):
    k = np.arange(M)
    i = np.arange(count)
    scale = np.where(k == 0, math.sqrt(1.0 / count), math.sqrt(2.0 / count))
    cos = scale * np.cos(np.pi / (2 * count) * ((k * (2 * i[:, None] + 1)) % (4 * count)))
    sin = (
        -2.0
        * scale
        * np.sin(np.pi * k / (2 * count))
        * np.sin(np.pi / count * ((k * (i[:, None] + 1)) % (2 * count)))
    )
    eigen = 2.0 - 2.0 * np.cos(np.pi * k / count)
    return cos, sin, eigen


def split(x):
    hi = x.astype(BF16)
    return hi, (x - hi.astype(F32)).astype(BF16)


def iota(shape, dim):
    return lax.broadcasted_iota(jnp.int32, shape, dim)


def first_kernel(
    dims,
    gx_hbm, gy_hbm, mask_hbm, off_ref, ty_hbm, tx_hbm,
    ts_ref, sp_ref,
    gx_ref, gy_ref, mask_ref, E, S, XA, XB, inv, ty, tx, part, pack, cols, r1, acc, r2, fin, acc2,
    in_sem, tab_sem, cs_send, cs_recv, rs_send, rs_recv,
    p1s, p1r, p2s, p2r, p3s, p3r, p4s, p4r,
):
    R, C, CH, TH, TW, screen = dims
    W = TW + LANES
    Q = W // LANES
    half = TH // 2
    group = lax.axis_index("groups")
    row = lax.axis_index("row")
    col = lax.axis_index("col")
    modes = CH * M
    crows = modes // C
    nparts = min(R, crows // 8)
    prow = crows // nparts

    def at(r, c):
        return (group, r, c)

    ty_copy = pltpu.make_async_copy(ty_hbm.at[pl.ds(col * TW, TW)], ty, tab_sem.at[0])
    tx_copy = pltpu.make_async_copy(tx_hbm.at[row], tx, tab_sem.at[1])
    loads = [
        pltpu.make_async_copy(src, dst, in_sem.at[i])
        for i, (src, dst) in enumerate(
            ((mask_hbm, mask_ref), (gx_hbm, gx_ref), (gy_hbm, gy_ref))
        )
    ]
    for cp in loads:
        cp.start()
    ty_copy.start()
    tx_copy.start()

    cols[...] = jnp.zeros_like(cols)
    E[:, 0:PAD, :] = jnp.zeros((2 * CH, PAD, W), F32)
    E[:, PAD + TH :, :] = jnp.zeros((2 * CH, PAD, W), F32)

    barrier = pltpu.get_barrier_semaphore()
    for off in range(1, C):
        pl.semaphore_signal(
            barrier, inc=1, device_id=at(row, lax.rem(col + off, C)), device_id_type=MESH
        )
    for off in range(1, R):
        pl.semaphore_signal(
            barrier, inc=1, device_id=at(lax.rem(row + off, R), col), device_id_type=MESH
        )

    below_row = jnp.minimum(row + 1, R - 1)
    right_col = jnp.minimum(col + 1, C - 1)
    stepx, stepy = [], []
    for c in range(CH):
        here = 0.25 * off_ref[c, row, col].astype(F32)
        stepx.append(0.25 * off_ref[c, below_row, col].astype(F32) - here)
        stepy.append(0.25 * off_ref[c, row, right_col].astype(F32) - here)
    ER = 32

    def edge_rows(t, carry):
        r0 = pl.multiple_of(t * ER, ER)
        rows = iota((ER, 1), 0) + r0
        lanes = iota((1, TW), 1)
        damp = 1.0 - 0.75 * mask_ref[pl.ds(r0, ER), :].astype(F32)
        last_row = (rows == TH - 1).astype(F32)
        last_col = (lanes == TW - 1).astype(F32)
        keep_row = jnp.where((rows == TH - 1) & (row == R - 1), 0.0, 1.0)
        keep_col = jnp.where((lanes == TW - 1) & (col == C - 1), 0.0, 1.0)
        b0 = pl.multiple_of(r0 + PAD, 8)
        for c in range(CH):
            ex = (gx_ref[c, pl.ds(r0, ER), :].astype(F32) * damp + last_row * stepx[c]) * keep_row
            ey = (gy_ref[c, pl.ds(r0, ER), :].astype(F32) * damp + last_col * stepy[c]) * keep_col
            E[c, pl.ds(b0, ER), 0:TW] = ex
            E[CH + c, pl.ds(b0, ER), 0:TW] = ey
        return carry

    for cp in loads:
        cp.wait()
    lax.fori_loop(0, TH // ER, edge_rows, 0)

    lane = iota((half, LANES), 1)
    for side in range(2):
        total = jnp.zeros((half, LANES), F32)
        for h in range(2):
            for a in range(2 * CH):
                rows = slice(PAD + h * half, PAD + (h + 1) * half)
                tile = slice(TW - LANES, TW) if side == 0 else slice(0, LANES)
                spot = 8 * a + 64 * h
                shift = (spot + (8 if side == 0 else 0)) % LANES
                x = E[a, rows, tile]
                if shift:
                    x = pltpu.roll(x, shift, 1)
                total = jnp.where((lane >= spot) & (lane < spot + 8), x, total)
        pack[side] = total

    pl.semaphore_wait(barrier, C - 1 + R - 1)
    to_right = pltpu.make_async_remote_copy(
        src_ref=pack.at[0], dst_ref=cols.at[0], send_sem=cs_send.at[0], recv_sem=cs_recv.at[0],
        device_id=at(row, jnp.minimum(col + 1, C - 1)), device_id_type=MESH,
    )
    to_left = pltpu.make_async_remote_copy(
        src_ref=pack.at[1], dst_ref=cols.at[1], send_sem=cs_send.at[1], recv_sem=cs_recv.at[1],
        device_id=at(row, jnp.maximum(col - 1, 0)), device_id_type=MESH,
    )
    pl.when(col < C - 1)(to_right.start)
    pl.when(col > 0)(to_left.start)

    IR = 32
    def inv_rows(t, carry):
        r0 = pl.multiple_of(t * IR, IR)
        places = iota((IR, 1), 0) + r0 - PAD + row * TH
        lanes = iota((1, W), 1)
        lanes = jnp.where(lanes < TW + 8, lanes, lanes - W) + col * TW
        crow = (places > 0).astype(F32) + (places < R * TH - 1).astype(F32)
        ccol = (lanes > 0).astype(F32) + (lanes < C * TW - 1).astype(F32)
        inside = ((places >= 0) & (places < R * TH)).astype(F32) * (
            (lanes >= 0) & (lanes < C * TW)
        ).astype(F32)
        inv[pl.ds(r0, IR), :] = inside / (screen + crow + ccol)
        return carry

    lax.fori_loop(0, (TH + 2 * PAD) // IR, inv_rows, 0)

    ty_copy.wait()
    tx_copy.wait()
    for c in range(CH):
        hs = []
        for d in range(2):
            e = E[d * CH + c, PAD : PAD + TH, 0:TW].astype(BF16)
            h = jnp.dot(e, ty[:, d * 2 * M : (d + 1) * 2 * M], preferred_element_type=F32)
            hs.append(h[:, :M] + h[:, M:])
        h = jnp.concatenate(hs, axis=0)
        hi, lo = split(h)
        o = jnp.dot(tx[...], jnp.concatenate([hi, lo], axis=1), preferred_element_type=F32)
        part[c * M : (c + 1) * M, :] = (o[:M, :M] + o[M:, :M]) + (o[:M, M:] + o[M:, M:])

    p1 = []
    for off in range(1, C):
        d = lax.rem(col + off, C)
        cp = pltpu.make_async_remote_copy(
            src_ref=part.at[pl.ds(pl.multiple_of(d * crows, 8), crows)], dst_ref=r1.at[off],
            send_sem=p1s.at[off], recv_sem=p1r.at[off],
            device_id=at(row, d), device_id_type=MESH,
        )
        cp.start()
        p1.append(cp)

    pl.when(col > 0)(to_right.wait_recv)
    pl.when(col < C - 1)(to_left.wait_recv)
    for a in range(2 * CH):
        for h in range(2):
            rows = slice(PAD + h * half, PAD + (h + 1) * half)
            spot = 8 * a + 64 * h
            left = pltpu.roll(cols[0], (120 - spot) % LANES, 1)
            right = cols[1]
            if spot:
                right = pltpu.roll(right, LANES - spot, 1)
            E[a, rows, TW:W] = jnp.where(lane < 8, right, jnp.where(lane >= 120, left, 0.0))
    to_below = pltpu.make_async_remote_copy(
        src_ref=E.at[:, pl.ds(PAD + TH - 8, 8), :], dst_ref=E.at[:, pl.ds(PAD - 8, 8), :],
        send_sem=rs_send.at[0], recv_sem=rs_recv.at[0],
        device_id=at(jnp.minimum(row + 1, R - 1), col), device_id_type=MESH,
    )
    to_above = pltpu.make_async_remote_copy(
        src_ref=E.at[:, pl.ds(PAD, 8), :], dst_ref=E.at[:, pl.ds(PAD + TH, 8), :],
        send_sem=rs_send.at[1], recv_sem=rs_recv.at[1],
        device_id=at(jnp.maximum(row - 1, 0), col), device_id_type=MESH,
    )
    pl.when(row < R - 1)(to_below.start)
    pl.when(row > 0)(to_above.start)

    for cp in p1:
        cp.wait_recv()
    total = part[pl.ds(pl.multiple_of(col * crows, 8), crows), :]
    for off in range(1, C):
        total = total + r1[off]
    acc[...] = total

    def guarded(cond, f):
        if nparts == R:
            f()
        else:
            pl.when(cond)(f)

    p2 = []
    for off in range(1, R):
        d = lax.rem(row + off, R)
        dd = jnp.minimum(d, nparts - 1) if nparts < R else d
        cp = pltpu.make_async_remote_copy(
            src_ref=acc.at[pl.ds(pl.multiple_of(dd * prow, 8), prow)], dst_ref=r2.at[off],
            send_sem=p2s.at[off], recv_sem=p2r.at[off],
            device_id=at(d, col), device_id_type=MESH,
        )
        guarded(d < nparts, cp.start)
        p2.append((cp, d))

    pl.when(row > 0)(to_below.wait_recv)
    pl.when(row < R - 1)(to_above.wait_recv)
    HR = 40
    nchunk = (TH + 16) // HR

    for buf in (XA, XB):
        buf[:, :, 0:8, :] = jnp.zeros((CH, Q, 8, LANES), F32)
        buf[:, :, PAD + TH + 8 :, :] = jnp.zeros((CH, Q, 8, LANES), F32)

    def source_rows(t, carry):
        b0 = pl.multiple_of(8 + t * HR, 8)
        d = inv[pl.ds(b0, HR), :]
        for c in range(CH):
            wide = E[c, pl.ds(pl.multiple_of(b0 - 8, 8), HR + 8), :]
            ey = E[CH + c, pl.ds(b0, HR), :]
            s = (wide[7 : 7 + HR] - wide[8:]) + (pltpu.roll(ey, 1, 1) - ey)
            s = s * d
            S[c, pl.ds(b0, HR), :] = s
            for q in range(Q):
                XA[c, q, pl.ds(b0, HR), :] = s[:, q * LANES : (q + 1) * LANES]
        return carry

    lax.fori_loop(0, nchunk, source_rows, 0)

    def neighbours(src, c, b0, count, tiles):
        at_rows = lambda by: pl.ds(b0 + by, count)
        lanes = iota((count, LANES), 1)
        mids = [src[c, q, at_rows(0), :] for q in range(Q)]
        back = [pltpu.roll(m, 1, 1) for m in mids]
        fore = [pltpu.roll(m, LANES - 1, 1) for m in mids]
        sums = []
        for q in range(tiles):
            before = jnp.where(lanes == 0, back[(q - 1) % Q], back[q])
            after = jnp.where(lanes == LANES - 1, fore[(q + 1) % Q], fore[q])
            sums.append(src[c, q, at_rows(-1), :] + src[c, q, at_rows(1), :] + (before + after))
        return sums

    def sweep(src, dst):
        def rows(t, carry):
            b0 = pl.multiple_of(8 + t * HR, 8)
            d = inv[pl.ds(b0, HR), :]
            for c in range(CH):
                for q, nb in enumerate(neighbours(src, c, b0, HR, Q)):
                    cut = slice(q * LANES, (q + 1) * LANES)
                    dst[c, q, pl.ds(b0, HR), :] = S[c, pl.ds(b0, HR), cut] + nb * d[:, cut]
            return carry

        lax.fori_loop(0, nchunk, rows, 0)

    sweep(XA, XB)
    sweep(XB, XA)

    for cp, d in p2:
        guarded(row < nparts, cp.wait_recv)
    me = jnp.minimum(row, nparts - 1) if nparts < R else row
    mine = pl.ds(pl.multiple_of(me * prow, 8), prow)

    def sum_rows():
        total = acc[mine, :]
        for off in range(1, R):
            total = total + r2[off]
        fin[...] = total
        acc2[mine, :] = total

    guarded(row < nparts, sum_rows)
    p3 = []
    for off in range(1, R):
        d = lax.rem(row + off, R)
        s = lax.rem(row + R - off, R)
        cp = pltpu.make_async_remote_copy(
            src_ref=fin, dst_ref=acc2.at[mine],
            send_sem=p3s.at[off], recv_sem=p3r.at[off],
            device_id=at(d, col), device_id_type=MESH,
        )
        guarded(row < nparts, cp.start)
        p3.append((cp, s))

    sweep(XA, XB)
    sweep(XB, XA)

    for cp, s in p3:
        guarded(s < nparts, cp.wait_recv)
    own = pl.ds(pl.multiple_of(col * crows, 8), crows)
    p4 = []
    for off in range(1, C):
        d = lax.rem(col + off, C)
        cp = pltpu.make_async_remote_copy(
            src_ref=acc2, dst_ref=sp_ref.at[own],
            send_sem=p4s.at[off], recv_sem=p4r.at[off],
            device_id=at(row, d), device_id_type=MESH,
        )
        cp.start()
        p4.append(cp)
    sp_ref[own, :] = acc2[...]

    sweep(XA, XB)
    sweep(XB, XA)
    LR = 32

    def last_rows(t, carry):
        b0 = pl.multiple_of(PAD + t * LR, 8)
        o0 = pl.multiple_of(t * LR, 8)
        d = inv[pl.ds(b0, LR), 0:TW]
        for c in range(CH):
            for q, nb in enumerate(neighbours(XA, c, b0, LR, Q - 1)):
                cut = slice(q * LANES, (q + 1) * LANES)
                ts_ref[c, pl.ds(o0, LR), cut] = S[c, pl.ds(b0, LR), cut] + nb * d[:, cut]
        return carry

    lax.fori_loop(0, TH // LR, last_rows, 0)

    for cp in p4:
        cp.wait_recv()
    pl.when(col < C - 1)(to_right.wait_send)
    pl.when(col > 0)(to_left.wait_send)
    pl.when(row < R - 1)(to_below.wait_send)
    pl.when(row > 0)(to_above.wait_send)
    for cp in p1:
        cp.wait_send()
    for cp, d in p2:
        guarded(d < nparts, cp.wait_send)
    for cp, d in p3:
        guarded(row < nparts, cp.wait_send)
    for cp in p4:
        cp.wait_send()


def last_kernel(
    dims,
    pos_ref, sp_ref, ts_ref, tb_ref, mu_ref, cxk_ref, cxr_ref, cyb_ref, cys_ref,
    out_ref, H, ends, sides,
):
    R, C, CH, TH, TW, screen = dims
    W = TH + LANES
    N = 16 * CH
    highest = lax.Precision.HIGHEST
    channel = pl.program_id(0)
    row, col = pos_ref[0], pos_ref[1]
    top, bottom = row == 0, row == R - 1
    left, right = col == 0, col == C - 1

    def coeffs(c):
        return sp_ref[c * M : (c + 1) * M, :] * tb_ref[0]

    @pl.when((channel == 0) & (top | bottom))
    def _():
        pick = jnp.where(
            top, cxr_ref[0:16, :].astype(F32), cxr_ref[TH - 16 : TH, :].astype(F32)
        )
        pick = pick[:, :M] + pick[:, M:]
        u = jnp.concatenate(
            [
                jnp.dot(pick, coeffs(c), precision=highest, preferred_element_type=F32)
                for c in range(CH)
            ],
            axis=0,
        )
        r = iota((N, M), 0) % 16
        edge = (top & (r == 0)) | (bottom & (r == 15))
        scale = 1.0 / (screen + jnp.where(edge, 3.0, 4.0))
        own = 2.0 - mu_ref[...]
        for _ in range(SWEEPS):
            up = jnp.where(r == 0, 0.0, pltpu.roll(u, 1, 0))
            down = jnp.where(r == 15, 0.0, pltpu.roll(u, N - 1, 0))
            u = (up + down + own * u) * scale
        ends[...] = u

    @pl.when((channel == 0) & (left | right))
    def _():
        cy = jnp.where(left, cys_ref[0:16, :], cys_ref[TW - 16 : TW, :])
        z = jnp.concatenate(
            [
                lax.dot_general(
                    cy, coeffs(c), (((1,), (1,)), ((), ())),
                    precision=highest, preferred_element_type=F32,
                )
                for c in range(CH)
            ],
            axis=0,
        )
        w = jnp.dot(z, cxk_ref[...], precision=highest, preferred_element_type=F32)
        r = iota((N, W), 0) % 16
        lanes = iota((N, W), 1)
        place = jnp.where(lanes < TH + 8, lanes, lanes - W) + row * TH
        inside = (place >= 0) & (place < R * TH)
        cx = (place > 0).astype(F32) + (place < R * TH - 1).astype(F32)
        edge = (left & (r == 0)) | (right & (r == 15))
        scale = jnp.where(inside, 1.0, 0.0) / (screen + cx + jnp.where(edge, 1.0, 2.0))
        w = jnp.where(inside, w, 0.0)
        for _ in range(SWEEPS):
            up = jnp.where(r == 0, 0.0, pltpu.roll(w, 1, 0))
            down = jnp.where(r == 15, 0.0, pltpu.roll(w, N - 1, 0))
            w = (up + down + (pltpu.roll(w, 1, 1) + pltpu.roll(w, W - 1, 1))) * scale
        wide = jnp.concatenate([w[:, 0:TH], jnp.zeros((LANES - N, TH), F32)], axis=0)
        sides[...] = wide.T

    moved = sp_ref[pl.ds(pl.multiple_of(channel * M, M), M), :] * tb_ref[1]
    hi, lo = split(moved)
    both = jnp.concatenate([hi, lo], axis=1)
    h = jnp.dot(cxr_ref[...], jnp.concatenate([both, both], axis=0), preferred_element_type=F32)
    H[...] = h[:, :M] + h[:, M:]

    @pl.when(top)
    def _():
        H[0:8, :] = ends[pl.ds(pl.multiple_of(channel * 16, 8), 8), :]

    @pl.when(bottom)
    def _():
        H[TH - 8 : TH, :] = ends[pl.ds(pl.multiple_of(channel * 16 + 8, 8), 8), :]

    hh, hl = split(H[...])
    lhs = jnp.concatenate([hh, hl, hh], axis=1)
    out_ref[0] = jnp.dot(lhs, cyb_ref[...], preferred_element_type=F32) + ts_ref[0]
    lane = iota((TH, LANES), 1)

    @pl.when(left)
    def _():
        turned = pltpu.roll(sides[...], lax.rem(LANES - 16 * channel, LANES), 1)
        ts = ts_ref[0, :, 0:LANES]
        out_ref[0, :, 0:LANES] = jnp.where(lane < 8, turned + ts, out_ref[0, :, 0:LANES])

    @pl.when(right)
    def _():
        turned = pltpu.roll(sides[...], LANES - 16 - 16 * channel, 1)
        ts = ts_ref[0, :, TW - LANES : TW]
        out_ref[0, :, TW - LANES : TW] = jnp.where(
            lane >= LANES - 8, turned + ts, out_ref[0, :, TW - LANES : TW]
        )


def body(grad_x, grad_y, seam_mask, tile_offset, tables):
    CH, TH, TW = grad_x.shape
    R = lax.axis_size("row")
    C = lax.axis_size("col")
    NX, NY = TH * R, TW * C
    screen = 0.5 * math.pi * math.pi / (NX * NY)
    dims = (R, C, CH, TH, TW, screen)
    W = TW + LANES
    modes = CH * M
    crows = modes // C
    nparts = min(R, crows // 8)
    prow = crows // nparts
    ty, tx, tb, mu, cxk, cxr, cyb, cys = tables
    vmem = pl.BlockSpec(memory_space=pltpu.VMEM)
    smem = pl.BlockSpec(memory_space=pltpu.SMEM)
    anys = pl.BlockSpec(memory_space=pl.ANY)
    rows = TH + 2 * PAD
    dma = pltpu.SemaphoreType.DMA
    ts, sp = pl.pallas_call(
        functools.partial(first_kernel, dims),
        out_shape=(
            jax.ShapeDtypeStruct((CH, TH, TW), F32),
            jax.ShapeDtypeStruct((modes, M), F32),
        ),
        in_specs=[anys, anys, anys, smem, anys, anys],
        out_specs=(vmem, vmem),
        scratch_shapes=[
            pltpu.VMEM((CH, TH, TW), BF16),
            pltpu.VMEM((CH, TH, TW), BF16),
            pltpu.VMEM((TH, TW), jnp.int32),
            pltpu.VMEM((2 * CH, rows, W), F32),
            pltpu.VMEM((CH, rows, W), F32),
            pltpu.VMEM((CH, W // LANES, rows, LANES), F32),
            pltpu.VMEM((CH, W // LANES, rows, LANES), F32),
            pltpu.VMEM((rows, W), F32),
            pltpu.VMEM((TW, 4 * M), BF16),
            pltpu.VMEM((2 * M, 2 * TH), BF16),
            pltpu.VMEM((modes, M), F32),
            pltpu.VMEM((2, TH // 2, LANES), F32),
            pltpu.VMEM((2, TH // 2, LANES), F32),
            pltpu.VMEM((C, crows, M), F32),
            pltpu.VMEM((crows, M), F32),
            pltpu.VMEM((R, prow, M), F32),
            pltpu.VMEM((prow, M), F32),
            pltpu.VMEM((crows, M), F32),
            dma((3,)), dma((2,)), dma((2,)), dma((2,)), dma((2,)), dma((2,)),
            dma((C,)), dma((C,)), dma((R,)), dma((R,)),
            dma((R,)), dma((R,)), dma((C,)), dma((C,)),
        ],
        compiler_params=pltpu.CompilerParams(
            collective_id=0, has_side_effects=True, vmem_limit_bytes=58 * 2**20
        ),
        name="sums_and_sweeps",
    )(grad_x, grad_y, seam_mask, tile_offset, ty, tx)

    pos = jnp.stack([lax.axis_index("row"), lax.axis_index("col")]).astype(jnp.int32)
    spec = pltpu.PrefetchScalarGridSpec(
        num_scalar_prefetch=1,
        grid=(CH,),
        in_specs=[
            pl.BlockSpec((modes, M), lambda i, p: (0, 0)),
            pl.BlockSpec((1, TH, TW), lambda i, p: (i, 0, 0)),
            pl.BlockSpec((2, M, M), lambda i, p: (0, 0, 0)),
            pl.BlockSpec((1, M), lambda i, p: (0, 0)),
            pl.BlockSpec((M, TH + LANES), lambda i, p: (p[0], 0)),
            pl.BlockSpec((TH, 2 * M), lambda i, p: (p[0], 0)),
            pl.BlockSpec((3 * M, TW), lambda i, p: (0, p[1])),
            pl.BlockSpec((TW, M), lambda i, p: (p[1], 0)),
        ],
        out_specs=pl.BlockSpec((1, TH, TW), lambda i, p: (i, 0, 0)),
        scratch_shapes=[
            pltpu.VMEM((TH, M), F32),
            pltpu.VMEM((16 * CH, M), F32),
            pltpu.VMEM((TH, LANES), F32),
        ],
    )
    return pl.pallas_call(
        functools.partial(last_kernel, dims),
        grid_spec=spec,
        out_shape=jax.ShapeDtypeStruct((CH, TH, TW), F32),
        compiler_params=pltpu.CompilerParams(vmem_limit_bytes=58 * 2**20),
        name="synthesis",
    )(pos, sp, ts, tb, mu, cxk, cxr, cyb, cys)


def solution(mesh):
    in_specs = (
        P(None, ("groups", "row"), "col"),
        P(None, ("groups", "row"), "col"),
        P(("groups", "row"), "col"),
        P(None, "groups", None),
        P(),
    )
    out_specs = P(None, ("groups", "row"), "col")
    R, C = mesh.shape["row"], mesh.shape["col"]
    G = mesh.shape["groups"]

    def whole(grad_x, grad_y, seam_mask, tile_offset):
        NX, NY = grad_x.shape[1] // G, grad_x.shape[2]
        TH, TW = NX // R, NY // C
        W = TH + LANES
        screen = 0.5 * math.pi * math.pi / (NX * NY)
        cx, sx, ex = np_tables(NX)
        cy, sy, ey = np_tables(NY)
        ty = np.concatenate(np_split(cy) + np_split(sy), axis=1)
        tiles = [
            np.concatenate([sx[r * TH : (r + 1) * TH].T, cx[r * TH : (r + 1) * TH].T], axis=1)
            for r in range(R)
        ]
        tx = np.stack([np.concatenate(np_split(t), axis=0) for t in tiles])
        lam = ex[:, None] + ey[None, :]
        tb = np.stack([1.0 / (screen + lam), ((4.0 - lam) / (4.0 + screen)) ** SWEEPS / (screen + lam)])
        cxk = np.zeros((R, M, W))
        for r in range(R):
            cxk[r, :, :TH] = cx[r * TH : (r + 1) * TH].T
            if r > 0:
                cxk[r, :, W - 8 :] = cx[r * TH - 8 : r * TH].T
            if r < R - 1:
                cxk[r, :, TH : TH + 8] = cx[(r + 1) * TH : (r + 1) * TH + 8].T
        cxr = np.concatenate(np_split(cx), axis=1)
        hi, lo = np_split(cy.T)
        cyb = np.concatenate([hi, hi, lo], axis=0)
        tables = (
            jnp.asarray(ty), jnp.asarray(tx),
            jnp.asarray(tb.astype(np.float32)),
            jnp.asarray(ey[None, :].astype(np.float32)),
            jnp.asarray(cxk.reshape(R * M, W).astype(np.float32)),
            jnp.asarray(cxr), jnp.asarray(cyb),
            jnp.asarray(cy.astype(np.float32)),
        )
        f = jax.shard_map(body, mesh=mesh, in_specs=in_specs, out_specs=out_specs, check_vma=False)
        return f(grad_x, grad_y, seam_mask, tile_offset, tables)

    return whole
```

```python
import functools
import math

import jax
import jax.numpy as jnp
import ml_dtypes
import numpy as np
from jax import lax
from jax.experimental import pallas as pl
from jax.experimental.pallas import tpu as pltpu
from jax.sharding import PartitionSpec as P

M = 128
SWEEPS = 8
LANES = 128
PAD = 16
MESH = pl.DeviceIdType.MESH
F32 = jnp.float32
BF16 = jnp.bfloat16


def np_split(x):
    hi = x.astype(np.float32).astype(ml_dtypes.bfloat16)
    lo = (x - hi.astype(np.float64)).astype(np.float32).astype(ml_dtypes.bfloat16)
    return hi, lo


def np_tables(count):
    k = np.arange(M)
    i = np.arange(count)
    scale = np.where(k == 0, math.sqrt(1.0 / count), math.sqrt(2.0 / count))
    cos = scale * np.cos(np.pi / (2 * count) * ((k * (2 * i[:, None] + 1)) % (4 * count)))
    sin = (
        -2.0
        * scale
        * np.sin(np.pi * k / (2 * count))
        * np.sin(np.pi / count * ((k * (i[:, None] + 1)) % (2 * count)))
    )
    eigen = 2.0 - 2.0 * np.cos(np.pi * k / count)
    return cos, sin, eigen


def split(x):
    hi = x.astype(BF16)
    return hi, (x - hi.astype(F32)).astype(BF16)


def iota(shape, dim):
    return lax.broadcasted_iota(jnp.int32, shape, dim)


def first_kernel(
    dims,
    gx_hbm, gy_hbm, mask_hbm, off_ref, ty_hbm, tx_hbm,
    ts_ref, sp_ref,
    gx_ref, gy_ref, mask_ref, E, S, XA, XB, inv, ty, tx, part, pack, cols, r1, acc, r2, fin, acc2,
    in_sem, tab_sem, cs_send, cs_recv, rs_send, rs_recv,
    p1s, p1r, p2s, p2r, p3s, p3r, p4s, p4r,
):
    R, C, CH, TH, TW, screen = dims
    W = TW + LANES
    Q = W // LANES
    half = TH // 2
    group = lax.axis_index("groups")
    row = lax.axis_index("row")
    col = lax.axis_index("col")
    modes = CH * M
    crows = modes // C
    nparts = min(R, crows // 8)
    prow = crows // nparts

    def at(r, c):
        return (group, r, c)

    ty_copy = pltpu.make_async_copy(ty_hbm.at[pl.ds(col * TW, TW)], ty, tab_sem.at[0])
    tx_copy = pltpu.make_async_copy(tx_hbm.at[row], tx, tab_sem.at[1])
    loads = [
        pltpu.make_async_copy(src, dst, in_sem.at[i])
        for i, (src, dst) in enumerate(
            ((mask_hbm, mask_ref), (gx_hbm, gx_ref), (gy_hbm, gy_ref))
        )
    ]
    for cp in loads:
        cp.start()
    ty_copy.start()
    tx_copy.start()

    cols[...] = jnp.zeros_like(cols)
    E[:, 0:PAD, :] = jnp.zeros((2 * CH, PAD, W), F32)
    E[:, PAD + TH :, :] = jnp.zeros((2 * CH, PAD, W), F32)

    barrier = pltpu.get_barrier_semaphore()
    for off in range(1, C):
        pl.semaphore_signal(
            barrier, inc=1, device_id=at(row, lax.rem(col + off, C)), device_id_type=MESH
        )
    for off in range(1, R):
        pl.semaphore_signal(
            barrier, inc=1, device_id=at(lax.rem(row + off, R), col), device_id_type=MESH
        )

    below_row = jnp.minimum(row + 1, R - 1)
    right_col = jnp.minimum(col + 1, C - 1)
    stepx, stepy = [], []
    for c in range(CH):
        here = 0.25 * off_ref[c, row, col].astype(F32)
        stepx.append(0.25 * off_ref[c, below_row, col].astype(F32) - here)
        stepy.append(0.25 * off_ref[c, row, right_col].astype(F32) - here)
    ER = 96

    def edge_rows(t, carry):
        r0 = pl.multiple_of(t * ER, ER)
        rows = iota((ER, 1), 0) + r0
        lanes = iota((1, TW), 1)
        damp = 1.0 - 0.75 * mask_ref[pl.ds(r0, ER), :].astype(F32)
        last_row = (rows == TH - 1).astype(F32)
        last_col = (lanes == TW - 1).astype(F32)
        keep_row = jnp.where((rows == TH - 1) & (row == R - 1), 0.0, 1.0)
        keep_col = jnp.where((lanes == TW - 1) & (col == C - 1), 0.0, 1.0)
        b0 = pl.multiple_of(r0 + PAD, 8)
        for c in range(CH):
            ex = (gx_ref[c, pl.ds(r0, ER), :].astype(F32) * damp + last_row * stepx[c]) * keep_row
            ey = (gy_ref[c, pl.ds(r0, ER), :].astype(F32) * damp + last_col * stepy[c]) * keep_col
            E[c, pl.ds(b0, ER), 0:TW] = ex
            E[CH + c, pl.ds(b0, ER), 0:TW] = ey
        return carry

    for cp in loads:
        cp.wait()
    lax.fori_loop(0, TH // ER, edge_rows, 0)

    lane = iota((half, LANES), 1)
    for side in range(2):
        total = jnp.zeros((half, LANES), F32)
        for h in range(2):
            for a in range(2 * CH):
                rows = slice(PAD + h * half, PAD + (h + 1) * half)
                tile = slice(TW - LANES, TW) if side == 0 else slice(0, LANES)
                spot = 8 * a + 64 * h
                shift = (spot + (8 if side == 0 else 0)) % LANES
                x = E[a, rows, tile]
                if shift:
                    x = pltpu.roll(x, shift, 1)
                total = jnp.where((lane >= spot) & (lane < spot + 8), x, total)
        pack[side] = total

    pl.semaphore_wait(barrier, C - 1 + R - 1)
    to_right = pltpu.make_async_remote_copy(
        src_ref=pack.at[0], dst_ref=cols.at[0], send_sem=cs_send.at[0], recv_sem=cs_recv.at[0],
        device_id=at(row, jnp.minimum(col + 1, C - 1)), device_id_type=MESH,
    )
    to_left = pltpu.make_async_remote_copy(
        src_ref=pack.at[1], dst_ref=cols.at[1], send_sem=cs_send.at[1], recv_sem=cs_recv.at[1],
        device_id=at(row, jnp.maximum(col - 1, 0)), device_id_type=MESH,
    )
    pl.when(col < C - 1)(to_right.start)
    pl.when(col > 0)(to_left.start)

    def row_copies(lanes, first):
        below = pltpu.make_async_remote_copy(
            src_ref=E.at[:, pl.ds(PAD + TH - 8, 8), lanes],
            dst_ref=E.at[:, pl.ds(PAD - 8, 8), lanes],
            send_sem=rs_send.at[first], recv_sem=rs_recv.at[first],
            device_id=at(jnp.minimum(row + 1, R - 1), col), device_id_type=MESH,
        )
        above = pltpu.make_async_remote_copy(
            src_ref=E.at[:, pl.ds(PAD, 8), lanes],
            dst_ref=E.at[:, pl.ds(PAD + TH, 8), lanes],
            send_sem=rs_send.at[first + 1], recv_sem=rs_recv.at[first + 1],
            device_id=at(jnp.maximum(row - 1, 0), col), device_id_type=MESH,
        )
        return below, above

    row_main = row_copies(pl.ds(0, TW), 0)
    row_corner = row_copies(pl.ds(TW, LANES), 2)

    pl.when(row < R - 1)(row_main[0].start)
    pl.when(row > 0)(row_main[1].start)

    IR = 104
    def inv_rows(t, carry):
        r0 = pl.multiple_of(t * IR, IR)
        places = iota((IR, 1), 0) + r0 - PAD + row * TH
        lanes = iota((1, W), 1)
        lanes = jnp.where(lanes < TW + 8, lanes, lanes - W) + col * TW
        crow = (places > 0).astype(F32) + (places < R * TH - 1).astype(F32)
        ccol = (lanes > 0).astype(F32) + (lanes < C * TW - 1).astype(F32)
        inside = ((places >= 0) & (places < R * TH)).astype(F32) * (
            (lanes >= 0) & (lanes < C * TW)
        ).astype(F32)
        inv[pl.ds(r0, IR), :] = inside / (screen + crow + ccol)
        return carry

    lax.fori_loop(0, (TH + 2 * PAD) // IR, inv_rows, 0)

    ty_copy.wait()
    tx_copy.wait()
    def forward(c):
        hs = []
        for d in range(2):
            e = E[d * CH + c, PAD : PAD + TH, 0:TW].astype(BF16)
            h = jnp.dot(e, ty[:, d * 2 * M : (d + 1) * 2 * M], preferred_element_type=F32)
            hs.append(h[:, :M] + h[:, M:])
        h = jnp.concatenate(hs, axis=0)
        hi, lo = split(h)
        o = jnp.dot(tx[...], jnp.concatenate([hi, lo], axis=1), preferred_element_type=F32)
        part[c * M : (c + 1) * M, :] = (o[:M, :M] + o[M:, :M]) + (o[:M, M:] + o[M:, M:])

    forward(0)

    pl.when(col > 0)(to_right.wait_recv)
    pl.when(col < C - 1)(to_left.wait_recv)
    for a in range(2 * CH):
        for h in range(2):
            rows = slice(PAD + h * half, PAD + (h + 1) * half)
            spot = 8 * a + 64 * h
            left = pltpu.roll(cols[0], (120 - spot) % LANES, 1)
            right = cols[1]
            if spot:
                right = pltpu.roll(right, LANES - spot, 1)
            E[a, rows, TW:W] = jnp.where(lane < 8, right, jnp.where(lane >= 120, left, 0.0))
    pl.when(row < R - 1)(row_corner[0].start)
    pl.when(row > 0)(row_corner[1].start)

    for c in range(1, CH):
        forward(c)

    p1 = []
    for off in range(1, C):
        d = lax.rem(col + off, C)
        cp = pltpu.make_async_remote_copy(
            src_ref=part.at[pl.ds(pl.multiple_of(d * crows, 8), crows)], dst_ref=r1.at[off],
            send_sem=p1s.at[off], recv_sem=p1r.at[off],
            device_id=at(row, d), device_id_type=MESH,
        )
        cp.start()
        p1.append(cp)

    for cp in p1:
        cp.wait_recv()
    total = part[pl.ds(pl.multiple_of(col * crows, 8), crows), :]
    for off in range(1, C):
        total = total + r1[off]
    acc[...] = total

    def guarded(cond, f):
        if nparts == R:
            f()
        else:
            pl.when(cond)(f)

    p2 = []
    for off in range(1, R):
        d = lax.rem(row + off, R)
        dd = jnp.minimum(d, nparts - 1) if nparts < R else d
        cp = pltpu.make_async_remote_copy(
            src_ref=acc.at[pl.ds(pl.multiple_of(dd * prow, 8), prow)], dst_ref=r2.at[off],
            send_sem=p2s.at[off], recv_sem=p2r.at[off],
            device_id=at(d, col), device_id_type=MESH,
        )
        guarded(d < nparts, cp.start)
        p2.append((cp, d))

    SR = 40
    HR = 40
    schunk = (TH + 16) // SR
    nchunk = (TH + 16) // HR

    for buf in (XA, XB):
        buf[:, :, 0:8, :] = jnp.zeros((CH, Q, 8, LANES), F32)
        buf[:, :, PAD + TH + 8 :, :] = jnp.zeros((CH, Q, 8, LANES), F32)

    def source_rows(t, carry):
        b0 = pl.multiple_of(8 + t * SR, 8)
        d = inv[pl.ds(b0, SR), :]
        for c in range(CH):
            wide = E[c, pl.ds(pl.multiple_of(b0 - 8, 8), SR + 8), :]
            ey = E[CH + c, pl.ds(b0, SR), :]
            s = (wide[7 : 7 + SR] - wide[8:]) + (pltpu.roll(ey, 1, 1) - ey)
            s = s * d
            S[c, pl.ds(b0, SR), :] = s
            for q in range(Q):
                XA[c, q, pl.ds(b0, SR), :] = s[:, q * LANES : (q + 1) * LANES]
        return carry

    lax.fori_loop(1, schunk - 1, source_rows, 0)
    for below, above in (row_main, row_corner):
        pl.when(row > 0)(below.wait_recv)
        pl.when(row < R - 1)(above.wait_recv)
    source_rows(0, 0)
    source_rows(schunk - 1, 0)

    def neighbours(src, c, b0, count, tiles):
        at_rows = lambda by: pl.ds(b0 + by, count)
        lanes = iota((count, LANES), 1)
        mids = [src[c, q, at_rows(0), :] for q in range(Q)]
        back = [pltpu.roll(m, 1, 1) for m in mids]
        fore = [pltpu.roll(m, LANES - 1, 1) for m in mids]
        sums = []
        for q in range(tiles):
            before = jnp.where(lanes == 0, back[(q - 1) % Q], back[q])
            after = jnp.where(lanes == LANES - 1, fore[(q + 1) % Q], fore[q])
            sums.append(src[c, q, at_rows(-1), :] + src[c, q, at_rows(1), :] + (before + after))
        return sums

    def sweep(src, dst):
        def one(c, carry):
            for t in range(nchunk):
                b0 = 8 + t * HR
                d = inv[b0 : b0 + HR, :]
                for q, nb in enumerate(neighbours(src, c, b0, HR, Q)):
                    cut = slice(q * LANES, (q + 1) * LANES)
                    dst[c, q, b0 : b0 + HR, :] = S[c, b0 : b0 + HR, cut] + nb * d[:, cut]
            return carry

        lax.fori_loop(0, CH, one, 0)

    sweep(XA, XB)
    sweep(XB, XA)

    for cp, d in p2:
        guarded(row < nparts, cp.wait_recv)
    me = jnp.minimum(row, nparts - 1) if nparts < R else row
    mine = pl.ds(pl.multiple_of(me * prow, 8), prow)

    def sum_rows():
        total = acc[mine, :]
        for off in range(1, R):
            total = total + r2[off]
        fin[...] = total
        acc2[mine, :] = total

    guarded(row < nparts, sum_rows)
    p3 = []
    for off in range(1, R):
        d = lax.rem(row + off, R)
        s = lax.rem(row + R - off, R)
        cp = pltpu.make_async_remote_copy(
            src_ref=fin, dst_ref=acc2.at[mine],
            send_sem=p3s.at[off], recv_sem=p3r.at[off],
            device_id=at(d, col), device_id_type=MESH,
        )
        guarded(row < nparts, cp.start)
        p3.append((cp, s))

    sweep(XA, XB)
    sweep(XB, XA)

    for cp, s in p3:
        guarded(s < nparts, cp.wait_recv)
    own = pl.ds(pl.multiple_of(col * crows, 8), crows)
    p4 = []
    for off in range(1, C):
        d = lax.rem(col + off, C)
        cp = pltpu.make_async_remote_copy(
            src_ref=acc2, dst_ref=sp_ref.at[own],
            send_sem=p4s.at[off], recv_sem=p4r.at[off],
            device_id=at(row, d), device_id_type=MESH,
        )
        cp.start()
        p4.append(cp)
    sp_ref[own, :] = acc2[...]

    sweep(XA, XB)
    sweep(XB, XA)
    LR = 48

    def last(c, carry):
        for t in range(TH // LR):
            b0 = PAD + t * LR
            d = inv[b0 : b0 + LR, 0:TW]
            for q, nb in enumerate(neighbours(XA, c, b0, LR, Q - 1)):
                cut = slice(q * LANES, (q + 1) * LANES)
                ts_ref[c, t * LR : (t + 1) * LR, cut] = (
                    S[c, b0 : b0 + LR, cut] + nb * d[:, cut]
                )
        return carry

    lax.fori_loop(0, CH, last, 0)

    for cp in p4:
        cp.wait_recv()
    pl.when(col < C - 1)(to_right.wait_send)
    pl.when(col > 0)(to_left.wait_send)
    for below, above in (row_main, row_corner):
        pl.when(row < R - 1)(below.wait_send)
        pl.when(row > 0)(above.wait_send)
    for cp in p1:
        cp.wait_send()
    for cp, d in p2:
        guarded(d < nparts, cp.wait_send)
    for cp, d in p3:
        guarded(row < nparts, cp.wait_send)
    for cp in p4:
        cp.wait_send()


def last_kernel(
    dims,
    pos_ref, sp_ref, ts_ref, tb_ref, mu_ref, cxk_ref, cxr_ref, cyb_ref, cys_ref,
    out_ref, H, ends, sides,
):
    R, C, CH, TH, TW, screen = dims
    W = TH + LANES
    N = 16 * CH
    highest = lax.Precision.HIGHEST
    channel = pl.program_id(0)
    row, col = pos_ref[0], pos_ref[1]
    top, bottom = row == 0, row == R - 1
    left, right = col == 0, col == C - 1

    def coeffs(c):
        return sp_ref[c * M : (c + 1) * M, :] * tb_ref[0]

    @pl.when((channel == 0) & (top | bottom))
    def _():
        pick = jnp.where(
            top, cxr_ref[0:16, :].astype(F32), cxr_ref[TH - 16 : TH, :].astype(F32)
        )
        pick = pick[:, :M] + pick[:, M:]
        u = jnp.concatenate(
            [
                jnp.dot(pick, coeffs(c), precision=highest, preferred_element_type=F32)
                for c in range(CH)
            ],
            axis=0,
        )
        r = iota((N, M), 0) % 16
        edge = (top & (r == 0)) | (bottom & (r == 15))
        scale = 1.0 / (screen + jnp.where(edge, 3.0, 4.0))
        own = 2.0 - mu_ref[...]
        for _ in range(SWEEPS):
            up = jnp.where(r == 0, 0.0, pltpu.roll(u, 1, 0))
            down = jnp.where(r == 15, 0.0, pltpu.roll(u, N - 1, 0))
            u = (up + down + own * u) * scale
        ends[...] = u

    @pl.when((channel == 0) & (left | right))
    def _():
        cy = jnp.where(left, cys_ref[0:16, :], cys_ref[TW - 16 : TW, :])
        z = jnp.concatenate(
            [
                lax.dot_general(
                    cy, coeffs(c), (((1,), (1,)), ((), ())),
                    precision=highest, preferred_element_type=F32,
                )
                for c in range(CH)
            ],
            axis=0,
        )
        w = jnp.dot(z, cxk_ref[...], precision=highest, preferred_element_type=F32)
        r = iota((N, W), 0) % 16
        lanes = iota((N, W), 1)
        place = jnp.where(lanes < TH + 8, lanes, lanes - W) + row * TH
        inside = (place >= 0) & (place < R * TH)
        cx = (place > 0).astype(F32) + (place < R * TH - 1).astype(F32)
        edge = (left & (r == 0)) | (right & (r == 15))
        scale = jnp.where(inside, 1.0, 0.0) / (screen + cx + jnp.where(edge, 1.0, 2.0))
        w = jnp.where(inside, w, 0.0)
        for _ in range(SWEEPS):
            up = jnp.where(r == 0, 0.0, pltpu.roll(w, 1, 0))
            down = jnp.where(r == 15, 0.0, pltpu.roll(w, N - 1, 0))
            w = (up + down + (pltpu.roll(w, 1, 1) + pltpu.roll(w, W - 1, 1))) * scale
        wide = jnp.concatenate([w[:, 0:TH], jnp.zeros((LANES - N, TH), F32)], axis=0)
        sides[...] = wide.T

    moved = sp_ref[pl.ds(pl.multiple_of(channel * M, M), M), :] * tb_ref[1]
    hi, lo = split(moved)
    both = jnp.concatenate([hi, lo], axis=1)
    h = jnp.dot(cxr_ref[...], jnp.concatenate([both, both], axis=0), preferred_element_type=F32)
    H[...] = h[:, :M] + h[:, M:]

    @pl.when(top)
    def _():
        H[0:8, :] = ends[pl.ds(pl.multiple_of(channel * 16, 8), 8), :]

    @pl.when(bottom)
    def _():
        H[TH - 8 : TH, :] = ends[pl.ds(pl.multiple_of(channel * 16 + 8, 8), 8), :]

    hh, hl = split(H[...])
    lhs = jnp.concatenate([hh, hl, hh], axis=1)
    out_ref[0] = jnp.dot(lhs, cyb_ref[...], preferred_element_type=F32) + ts_ref[0]
    lane = iota((TH, LANES), 1)

    @pl.when(left)
    def _():
        turned = pltpu.roll(sides[...], lax.rem(LANES - 16 * channel, LANES), 1)
        ts = ts_ref[0, :, 0:LANES]
        out_ref[0, :, 0:LANES] = jnp.where(lane < 8, turned + ts, out_ref[0, :, 0:LANES])

    @pl.when(right)
    def _():
        turned = pltpu.roll(sides[...], LANES - 16 - 16 * channel, 1)
        ts = ts_ref[0, :, TW - LANES : TW]
        out_ref[0, :, TW - LANES : TW] = jnp.where(
            lane >= LANES - 8, turned + ts, out_ref[0, :, TW - LANES : TW]
        )


def body(grad_x, grad_y, seam_mask, tile_offset, tables):
    CH, TH, TW = grad_x.shape
    R = lax.axis_size("row")
    C = lax.axis_size("col")
    NX, NY = TH * R, TW * C
    screen = 0.5 * math.pi * math.pi / (NX * NY)
    dims = (R, C, CH, TH, TW, screen)
    W = TW + LANES
    modes = CH * M
    crows = modes // C
    nparts = min(R, crows // 8)
    prow = crows // nparts
    ty, tx, tb, mu, cxk, cxr, cyb, cys = tables
    vmem = pl.BlockSpec(memory_space=pltpu.VMEM)
    smem = pl.BlockSpec(memory_space=pltpu.SMEM)
    anys = pl.BlockSpec(memory_space=pl.ANY)
    rows = TH + 2 * PAD
    dma = pltpu.SemaphoreType.DMA
    ts, sp = pl.pallas_call(
        functools.partial(first_kernel, dims),
        out_shape=(
            jax.ShapeDtypeStruct((CH, TH, TW), F32),
            jax.ShapeDtypeStruct((modes, M), F32),
        ),
        in_specs=[anys, anys, anys, smem, anys, anys],
        out_specs=(vmem, vmem),
        scratch_shapes=[
            pltpu.VMEM((CH, TH, TW), BF16),
            pltpu.VMEM((CH, TH, TW), BF16),
            pltpu.VMEM((TH, TW), jnp.int32),
            pltpu.VMEM((2 * CH, rows, W), F32),
            pltpu.VMEM((CH, rows, W), F32),
            pltpu.VMEM((CH, W // LANES, rows, LANES), F32),
            pltpu.VMEM((CH, W // LANES, rows, LANES), F32),
            pltpu.VMEM((rows, W), F32),
            pltpu.VMEM((TW, 4 * M), BF16),
            pltpu.VMEM((2 * M, 2 * TH), BF16),
            pltpu.VMEM((modes, M), F32),
            pltpu.VMEM((2, TH // 2, LANES), F32),
            pltpu.VMEM((2, TH // 2, LANES), F32),
            pltpu.VMEM((C, crows, M), F32),
            pltpu.VMEM((crows, M), F32),
            pltpu.VMEM((R, prow, M), F32),
            pltpu.VMEM((prow, M), F32),
            pltpu.VMEM((crows, M), F32),
            dma((3,)), dma((2,)), dma((2,)), dma((2,)), dma((4,)), dma((4,)),
            dma((C,)), dma((C,)), dma((R,)), dma((R,)),
            dma((R,)), dma((R,)), dma((C,)), dma((C,)),
        ],
        compiler_params=pltpu.CompilerParams(
            collective_id=0, has_side_effects=True, vmem_limit_bytes=58 * 2**20
        ),
        name="sums_and_sweeps",
    )(grad_x, grad_y, seam_mask, tile_offset, ty, tx)

    pos = jnp.stack([lax.axis_index("row"), lax.axis_index("col")]).astype(jnp.int32)
    spec = pltpu.PrefetchScalarGridSpec(
        num_scalar_prefetch=1,
        grid=(CH,),
        in_specs=[
            pl.BlockSpec((modes, M), lambda i, p: (0, 0)),
            pl.BlockSpec((1, TH, TW), lambda i, p: (i, 0, 0)),
            pl.BlockSpec((2, M, M), lambda i, p: (0, 0, 0)),
            pl.BlockSpec((1, M), lambda i, p: (0, 0)),
            pl.BlockSpec((M, TH + LANES), lambda i, p: (p[0], 0)),
            pl.BlockSpec((TH, 2 * M), lambda i, p: (p[0], 0)),
            pl.BlockSpec((3 * M, TW), lambda i, p: (0, p[1])),
            pl.BlockSpec((TW, M), lambda i, p: (p[1], 0)),
        ],
        out_specs=pl.BlockSpec((1, TH, TW), lambda i, p: (i, 0, 0)),
        scratch_shapes=[
            pltpu.VMEM((TH, M), F32),
            pltpu.VMEM((16 * CH, M), F32),
            pltpu.VMEM((TH, LANES), F32),
        ],
    )
    return pl.pallas_call(
        functools.partial(last_kernel, dims),
        grid_spec=spec,
        out_shape=jax.ShapeDtypeStruct((CH, TH, TW), F32),
        compiler_params=pltpu.CompilerParams(vmem_limit_bytes=58 * 2**20),
        name="synthesis",
    )(pos, sp, ts, tb, mu, cxk, cxr, cyb, cys)


def solution(mesh):
    in_specs = (
        P(None, ("groups", "row"), "col"),
        P(None, ("groups", "row"), "col"),
        P(("groups", "row"), "col"),
        P(None, "groups", None),
        P(),
    )
    out_specs = P(None, ("groups", "row"), "col")
    R, C = mesh.shape["row"], mesh.shape["col"]
    G = mesh.shape["groups"]

    def whole(grad_x, grad_y, seam_mask, tile_offset):
        NX, NY = grad_x.shape[1] // G, grad_x.shape[2]
        TH, TW = NX // R, NY // C
        W = TH + LANES
        screen = 0.5 * math.pi * math.pi / (NX * NY)
        cx, sx, ex = np_tables(NX)
        cy, sy, ey = np_tables(NY)
        ty = np.concatenate(np_split(cy) + np_split(sy), axis=1)
        tiles = [
            np.concatenate([sx[r * TH : (r + 1) * TH].T, cx[r * TH : (r + 1) * TH].T], axis=1)
            for r in range(R)
        ]
        tx = np.stack([np.concatenate(np_split(t), axis=0) for t in tiles])
        lam = ex[:, None] + ey[None, :]
        tb = np.stack([1.0 / (screen + lam), ((4.0 - lam) / (4.0 + screen)) ** SWEEPS / (screen + lam)])
        cxk = np.zeros((R, M, W))
        for r in range(R):
            cxk[r, :, :TH] = cx[r * TH : (r + 1) * TH].T
            if r > 0:
                cxk[r, :, W - 8 :] = cx[r * TH - 8 : r * TH].T
            if r < R - 1:
                cxk[r, :, TH : TH + 8] = cx[(r + 1) * TH : (r + 1) * TH + 8].T
        cxr = np.concatenate(np_split(cx), axis=1)
        hi, lo = np_split(cy.T)
        cyb = np.concatenate([hi, hi, lo], axis=0)
        tables = (
            jnp.asarray(ty), jnp.asarray(tx),
            jnp.asarray(tb.astype(np.float32)),
            jnp.asarray(ey[None, :].astype(np.float32)),
            jnp.asarray(cxk.reshape(R * M, W).astype(np.float32)),
            jnp.asarray(cxr), jnp.asarray(cyb),
            jnp.asarray(cy.astype(np.float32)),
        )
        f = jax.shard_map(body, mesh=mesh, in_specs=in_specs, out_specs=out_specs, check_vma=False)
        return f(grad_x, grad_y, seam_mask, tile_offset, tables)

    return whole
```

```python
import functools
import math

import jax
import jax.numpy as jnp
import ml_dtypes
import numpy as np
from jax import lax
from jax.experimental import pallas as pl
from jax.experimental.pallas import tpu as pltpu
from jax.sharding import PartitionSpec as P

M = 128
SWEEPS = 8
LANES = 128
PAD = 16
MESH = pl.DeviceIdType.MESH
F32 = jnp.float32
BF16 = jnp.bfloat16


def np_split(x):
    hi = x.astype(np.float32).astype(ml_dtypes.bfloat16)
    lo = (x - hi.astype(np.float64)).astype(np.float32).astype(ml_dtypes.bfloat16)
    return hi, lo


def np_tables(count):
    k = np.arange(M)
    i = np.arange(count)
    scale = np.where(k == 0, math.sqrt(1.0 / count), math.sqrt(2.0 / count))
    cos = scale * np.cos(np.pi / (2 * count) * ((k * (2 * i[:, None] + 1)) % (4 * count)))
    sin = (
        -2.0
        * scale
        * np.sin(np.pi * k / (2 * count))
        * np.sin(np.pi / count * ((k * (i[:, None] + 1)) % (2 * count)))
    )
    eigen = 2.0 - 2.0 * np.cos(np.pi * k / count)
    return cos, sin, eigen


def split(x):
    hi = x.astype(BF16)
    return hi, (x - hi.astype(F32)).astype(BF16)


def iota(shape, dim):
    return lax.broadcasted_iota(jnp.int32, shape, dim)


def first_kernel(
    dims,
    gx_hbm, gy_hbm, mask_hbm, off_ref, ty_hbm, tx_hbm,
    ts_ref, sp_ref,
    gx_ref, gy_ref, mask_ref, E, S, XA, XB, inv, ty, tx, part, pack, cols, r1, acc, r2, fin, acc2,
    in_sem, tab_sem, cs_send, cs_recv, rs_send, rs_recv,
    p1s, p1r, p2s, p2r, p3s, p3r, p4s, p4r,
):
    R, C, CH, TH, TW, screen = dims
    W = TW + LANES
    Q = W // LANES
    half = TH // 2
    group = lax.axis_index("groups")
    row = lax.axis_index("row")
    col = lax.axis_index("col")
    modes = CH * M
    crows = modes // C
    nparts = min(R, crows // 8)
    prow = crows // nparts

    def at(r, c):
        return (group, r, c)

    ty_copy = pltpu.make_async_copy(ty_hbm.at[pl.ds(col * TW, TW)], ty, tab_sem.at[0])
    tx_copy = pltpu.make_async_copy(tx_hbm.at[row], tx, tab_sem.at[1])
    loads = [
        pltpu.make_async_copy(src, dst, in_sem.at[i])
        for i, (src, dst) in enumerate(
            ((mask_hbm, mask_ref), (gx_hbm, gx_ref), (gy_hbm, gy_ref))
        )
    ]
    for cp in loads:
        cp.start()
    ty_copy.start()
    tx_copy.start()

    cols[...] = jnp.zeros_like(cols)
    E[:, 0:PAD, :] = jnp.zeros((2 * CH, PAD, W), F32)
    E[:, PAD + TH :, :] = jnp.zeros((2 * CH, PAD, W), F32)

    barrier = pltpu.get_barrier_semaphore()
    for off in range(1, C):
        pl.semaphore_signal(
            barrier, inc=1, device_id=at(row, lax.rem(col + off, C)), device_id_type=MESH
        )
    for off in range(1, R):
        pl.semaphore_signal(
            barrier, inc=1, device_id=at(lax.rem(row + off, R), col), device_id_type=MESH
        )

    below_row = jnp.minimum(row + 1, R - 1)
    right_col = jnp.minimum(col + 1, C - 1)
    stepx, stepy = [], []
    for c in range(CH):
        here = 0.25 * off_ref[c, row, col].astype(F32)
        stepx.append(0.25 * off_ref[c, below_row, col].astype(F32) - here)
        stepy.append(0.25 * off_ref[c, row, right_col].astype(F32) - here)
    ER = 96

    def edge_rows(t, carry):
        r0 = pl.multiple_of(t * ER, ER)
        rows = iota((ER, 1), 0) + r0
        lanes = iota((1, TW), 1)
        damp = 1.0 - 0.75 * mask_ref[pl.ds(r0, ER), :].astype(F32)
        last_row = (rows == TH - 1).astype(F32)
        last_col = (lanes == TW - 1).astype(F32)
        keep_row = jnp.where((rows == TH - 1) & (row == R - 1), 0.0, 1.0)
        keep_col = jnp.where((lanes == TW - 1) & (col == C - 1), 0.0, 1.0)
        b0 = pl.multiple_of(r0 + PAD, 8)
        for c in range(CH):
            ex = (gx_ref[c, pl.ds(r0, ER), :].astype(F32) * damp + last_row * stepx[c]) * keep_row
            ey = (gy_ref[c, pl.ds(r0, ER), :].astype(F32) * damp + last_col * stepy[c]) * keep_col
            E[c, pl.ds(b0, ER), 0:TW] = ex
            E[CH + c, pl.ds(b0, ER), 0:TW] = ey
        return carry

    for cp in loads:
        cp.wait()
    lax.fori_loop(0, TH // ER, edge_rows, 0)

    lane = iota((half, LANES), 1)
    for side in range(2):
        total = jnp.zeros((half, LANES), F32)
        for h in range(2):
            for a in range(2 * CH):
                rows = slice(PAD + h * half, PAD + (h + 1) * half)
                tile = slice(TW - LANES, TW) if side == 0 else slice(0, LANES)
                spot = 8 * a + 64 * h
                shift = (spot + (8 if side == 0 else 0)) % LANES
                x = E[a, rows, tile]
                if shift:
                    x = pltpu.roll(x, shift, 1)
                total = jnp.where((lane >= spot) & (lane < spot + 8), x, total)
        pack[side] = total

    pl.semaphore_wait(barrier, C - 1 + R - 1)
    to_right = pltpu.make_async_remote_copy(
        src_ref=pack.at[0], dst_ref=cols.at[0], send_sem=cs_send.at[0], recv_sem=cs_recv.at[0],
        device_id=at(row, jnp.minimum(col + 1, C - 1)), device_id_type=MESH,
    )
    to_left = pltpu.make_async_remote_copy(
        src_ref=pack.at[1], dst_ref=cols.at[1], send_sem=cs_send.at[1], recv_sem=cs_recv.at[1],
        device_id=at(row, jnp.maximum(col - 1, 0)), device_id_type=MESH,
    )
    pl.when(col < C - 1)(to_right.start)
    pl.when(col > 0)(to_left.start)

    def row_copies(lanes, first):
        below = pltpu.make_async_remote_copy(
            src_ref=E.at[:, pl.ds(PAD + TH - 8, 8), lanes],
            dst_ref=E.at[:, pl.ds(PAD - 8, 8), lanes],
            send_sem=rs_send.at[first], recv_sem=rs_recv.at[first],
            device_id=at(jnp.minimum(row + 1, R - 1), col), device_id_type=MESH,
        )
        above = pltpu.make_async_remote_copy(
            src_ref=E.at[:, pl.ds(PAD, 8), lanes],
            dst_ref=E.at[:, pl.ds(PAD + TH, 8), lanes],
            send_sem=rs_send.at[first + 1], recv_sem=rs_recv.at[first + 1],
            device_id=at(jnp.maximum(row - 1, 0), col), device_id_type=MESH,
        )
        return below, above

    row_main = row_copies(pl.ds(0, TW), 0)
    row_corner = row_copies(pl.ds(TW, LANES), 2)

    pl.when(row < R - 1)(row_main[0].start)
    pl.when(row > 0)(row_main[1].start)

    ty_copy.wait()
    tx_copy.wait()
    def forward(c):
        hs = []
        for d in range(2):
            e = E[d * CH + c, PAD : PAD + TH, 0:TW].astype(BF16)
            h = jnp.dot(e, ty[:, d * 2 * M : (d + 1) * 2 * M], preferred_element_type=F32)
            hs.append(h[:, :M] + h[:, M:])
        h = jnp.concatenate(hs, axis=0)
        hi, lo = split(h)
        o = jnp.dot(tx[...], jnp.concatenate([hi, lo], axis=1), preferred_element_type=F32)
        part[c * M : (c + 1) * M, :] = (o[:M, :M] + o[M:, :M]) + (o[:M, M:] + o[M:, M:])

    for c in range(CH):
        forward(c)

    p1 = []
    for off in range(1, C):
        d = lax.rem(col + off, C)
        cp = pltpu.make_async_remote_copy(
            src_ref=part.at[pl.ds(pl.multiple_of(d * crows, 8), crows)], dst_ref=r1.at[off],
            send_sem=p1s.at[off], recv_sem=p1r.at[off],
            device_id=at(row, d), device_id_type=MESH,
        )
        cp.start()
        p1.append(cp)

    IR = 104
    def inv_rows(t, carry):
        r0 = pl.multiple_of(t * IR, IR)
        places = iota((IR, 1), 0) + r0 - PAD + row * TH
        lanes = iota((1, W), 1)
        lanes = jnp.where(lanes < TW + 8, lanes, lanes - W) + col * TW
        crow = (places > 0).astype(F32) + (places < R * TH - 1).astype(F32)
        ccol = (lanes > 0).astype(F32) + (lanes < C * TW - 1).astype(F32)
        inside = ((places >= 0) & (places < R * TH)).astype(F32) * (
            (lanes >= 0) & (lanes < C * TW)
        ).astype(F32)
        inv[pl.ds(r0, IR), :] = inside / (screen + crow + ccol)
        return carry

    lax.fori_loop(0, (TH + 2 * PAD) // IR, inv_rows, 0)

    pl.when(col > 0)(to_right.wait_recv)
    pl.when(col < C - 1)(to_left.wait_recv)
    for a in range(2 * CH):
        for h in range(2):
            rows = slice(PAD + h * half, PAD + (h + 1) * half)
            spot = 8 * a + 64 * h
            left = pltpu.roll(cols[0], (120 - spot) % LANES, 1)
            right = cols[1]
            if spot:
                right = pltpu.roll(right, LANES - spot, 1)
            E[a, rows, TW:W] = jnp.where(lane < 8, right, jnp.where(lane >= 120, left, 0.0))
    pl.when(row < R - 1)(row_corner[0].start)
    pl.when(row > 0)(row_corner[1].start)

    for cp in p1:
        cp.wait_recv()
    total = part[pl.ds(pl.multiple_of(col * crows, 8), crows), :]
    for off in range(1, C):
        total = total + r1[off]
    acc[...] = total

    def guarded(cond, f):
        if nparts == R:
            f()
        else:
            pl.when(cond)(f)

    p2 = []
    for off in range(1, R):
        d = lax.rem(row + off, R)
        dd = jnp.minimum(d, nparts - 1) if nparts < R else d
        cp = pltpu.make_async_remote_copy(
            src_ref=acc.at[pl.ds(pl.multiple_of(dd * prow, 8), prow)], dst_ref=r2.at[off],
            send_sem=p2s.at[off], recv_sem=p2r.at[off],
            device_id=at(d, col), device_id_type=MESH,
        )
        guarded(d < nparts, cp.start)
        p2.append((cp, d))

    SR = 40
    HR = 40
    schunk = (TH + 16) // SR
    nchunk = (TH + 16) // HR

    for buf in (XA, XB):
        buf[:, :, 0:8, :] = jnp.zeros((CH, Q, 8, LANES), F32)
        buf[:, :, PAD + TH + 8 :, :] = jnp.zeros((CH, Q, 8, LANES), F32)

    def source_rows(t, carry):
        b0 = pl.multiple_of(8 + t * SR, 8)
        d = inv[pl.ds(b0, SR), :]
        for c in range(CH):
            wide = E[c, pl.ds(pl.multiple_of(b0 - 8, 8), SR + 8), :]
            ey = E[CH + c, pl.ds(b0, SR), :]
            s = (wide[7 : 7 + SR] - wide[8:]) + (pltpu.roll(ey, 1, 1) - ey)
            s = s * d
            S[c, pl.ds(b0, SR), :] = s
            for q in range(Q):
                XA[c, q, pl.ds(b0, SR), :] = s[:, q * LANES : (q + 1) * LANES]
        return carry

    lax.fori_loop(1, schunk - 1, source_rows, 0)
    for below, above in (row_main, row_corner):
        pl.when(row > 0)(below.wait_recv)
        pl.when(row < R - 1)(above.wait_recv)
    source_rows(0, 0)
    source_rows(schunk - 1, 0)

    def neighbours(src, c, b0, count, tiles):
        at_rows = lambda by: pl.ds(b0 + by, count)
        lanes = iota((count, LANES), 1)
        mids = [src[c, q, at_rows(0), :] for q in range(Q)]
        back = [pltpu.roll(m, 1, 1) for m in mids]
        fore = [pltpu.roll(m, LANES - 1, 1) for m in mids]
        sums = []
        for q in range(tiles):
            before = jnp.where(lanes == 0, back[(q - 1) % Q], back[q])
            after = jnp.where(lanes == LANES - 1, fore[(q + 1) % Q], fore[q])
            sums.append(src[c, q, at_rows(-1), :] + src[c, q, at_rows(1), :] + (before + after))
        return sums

    def sweep(src, dst):
        def one(c, carry):
            for t in range(nchunk):
                b0 = 8 + t * HR
                d = inv[b0 : b0 + HR, :]
                for q, nb in enumerate(neighbours(src, c, b0, HR, Q)):
                    cut = slice(q * LANES, (q + 1) * LANES)
                    dst[c, q, b0 : b0 + HR, :] = S[c, b0 : b0 + HR, cut] + nb * d[:, cut]
            return carry

        lax.fori_loop(0, CH, one, 0)

    sweep(XA, XB)
    sweep(XB, XA)

    for cp, d in p2:
        guarded(row < nparts, cp.wait_recv)
    me = jnp.minimum(row, nparts - 1) if nparts < R else row
    mine = pl.ds(pl.multiple_of(me * prow, 8), prow)

    def sum_rows():
        total = acc[mine, :]
        for off in range(1, R):
            total = total + r2[off]
        fin[...] = total
        acc2[mine, :] = total

    guarded(row < nparts, sum_rows)
    p3 = []
    for off in range(1, R):
        d = lax.rem(row + off, R)
        s = lax.rem(row + R - off, R)
        cp = pltpu.make_async_remote_copy(
            src_ref=fin, dst_ref=acc2.at[mine],
            send_sem=p3s.at[off], recv_sem=p3r.at[off],
            device_id=at(d, col), device_id_type=MESH,
        )
        guarded(row < nparts, cp.start)
        p3.append((cp, s))

    sweep(XA, XB)
    sweep(XB, XA)

    for cp, s in p3:
        guarded(s < nparts, cp.wait_recv)
    own = pl.ds(pl.multiple_of(col * crows, 8), crows)
    p4 = []
    for off in range(1, C):
        d = lax.rem(col + off, C)
        cp = pltpu.make_async_remote_copy(
            src_ref=acc2, dst_ref=sp_ref.at[own],
            send_sem=p4s.at[off], recv_sem=p4r.at[off],
            device_id=at(row, d), device_id_type=MESH,
        )
        cp.start()
        p4.append(cp)
    sp_ref[own, :] = acc2[...]

    sweep(XA, XB)
    sweep(XB, XA)
    LR = 48

    def last(c, carry):
        for t in range(TH // LR):
            b0 = PAD + t * LR
            d = inv[b0 : b0 + LR, 0:TW]
            for q, nb in enumerate(neighbours(XA, c, b0, LR, Q - 1)):
                cut = slice(q * LANES, (q + 1) * LANES)
                ts_ref[c, t * LR : (t + 1) * LR, cut] = (
                    S[c, b0 : b0 + LR, cut] + nb * d[:, cut]
                )
        return carry

    lax.fori_loop(0, CH, last, 0)

    for cp in p4:
        cp.wait_recv()
    pl.when(col < C - 1)(to_right.wait_send)
    pl.when(col > 0)(to_left.wait_send)
    for below, above in (row_main, row_corner):
        pl.when(row < R - 1)(below.wait_send)
        pl.when(row > 0)(above.wait_send)
    for cp in p1:
        cp.wait_send()
    for cp, d in p2:
        guarded(d < nparts, cp.wait_send)
    for cp, d in p3:
        guarded(row < nparts, cp.wait_send)
    for cp in p4:
        cp.wait_send()


def last_kernel(
    dims,
    pos_ref, sp_ref, ts_ref, tb_ref, mu_ref, cxk_ref, cxr_ref, cyb_ref, cys_ref,
    out_ref, H, ends, sides,
):
    R, C, CH, TH, TW, screen = dims
    W = TH + LANES
    N = 16 * CH
    highest = lax.Precision.HIGHEST
    channel = pl.program_id(0)
    row, col = pos_ref[0], pos_ref[1]
    top, bottom = row == 0, row == R - 1
    left, right = col == 0, col == C - 1

    def coeffs(c):
        return sp_ref[c * M : (c + 1) * M, :] * tb_ref[0]

    @pl.when((channel == 0) & (top | bottom))
    def _():
        pick = jnp.where(
            top, cxr_ref[0:16, :].astype(F32), cxr_ref[TH - 16 : TH, :].astype(F32)
        )
        pick = pick[:, :M] + pick[:, M:]
        u = jnp.concatenate(
            [
                jnp.dot(pick, coeffs(c), precision=highest, preferred_element_type=F32)
                for c in range(CH)
            ],
            axis=0,
        )
        r = iota((N, M), 0) % 16
        edge = (top & (r == 0)) | (bottom & (r == 15))
        scale = 1.0 / (screen + jnp.where(edge, 3.0, 4.0))
        own = 2.0 - mu_ref[...]
        for _ in range(SWEEPS):
            up = jnp.where(r == 0, 0.0, pltpu.roll(u, 1, 0))
            down = jnp.where(r == 15, 0.0, pltpu.roll(u, N - 1, 0))
            u = (up + down + own * u) * scale
        ends[...] = u

    @pl.when((channel == 0) & (left | right))
    def _():
        cy = jnp.where(left, cys_ref[0:16, :], cys_ref[TW - 16 : TW, :])
        z = jnp.concatenate(
            [
                lax.dot_general(
                    cy, coeffs(c), (((1,), (1,)), ((), ())),
                    precision=highest, preferred_element_type=F32,
                )
                for c in range(CH)
            ],
            axis=0,
        )
        w = jnp.dot(z, cxk_ref[...], precision=highest, preferred_element_type=F32)
        r = iota((N, W), 0) % 16
        lanes = iota((N, W), 1)
        place = jnp.where(lanes < TH + 8, lanes, lanes - W) + row * TH
        inside = (place >= 0) & (place < R * TH)
        cx = (place > 0).astype(F32) + (place < R * TH - 1).astype(F32)
        edge = (left & (r == 0)) | (right & (r == 15))
        scale = jnp.where(inside, 1.0, 0.0) / (screen + cx + jnp.where(edge, 1.0, 2.0))
        w = jnp.where(inside, w, 0.0)
        for _ in range(SWEEPS):
            up = jnp.where(r == 0, 0.0, pltpu.roll(w, 1, 0))
            down = jnp.where(r == 15, 0.0, pltpu.roll(w, N - 1, 0))
            w = (up + down + (pltpu.roll(w, 1, 1) + pltpu.roll(w, W - 1, 1))) * scale
        wide = jnp.concatenate([w[:, 0:TH], jnp.zeros((LANES - N, TH), F32)], axis=0)
        sides[...] = wide.T

    moved = sp_ref[pl.ds(pl.multiple_of(channel * M, M), M), :] * tb_ref[1]
    hi, lo = split(moved)
    both = jnp.concatenate([hi, lo], axis=1)
    h = jnp.dot(cxr_ref[...], jnp.concatenate([both, both], axis=0), preferred_element_type=F32)
    H[...] = h[:, :M] + h[:, M:]

    @pl.when(top)
    def _():
        H[0:8, :] = ends[pl.ds(pl.multiple_of(channel * 16, 8), 8), :]

    @pl.when(bottom)
    def _():
        H[TH - 8 : TH, :] = ends[pl.ds(pl.multiple_of(channel * 16 + 8, 8), 8), :]

    hh, hl = split(H[...])
    lhs = jnp.concatenate([hh, hl, hh], axis=1)
    out_ref[0] = jnp.dot(lhs, cyb_ref[...], preferred_element_type=F32) + ts_ref[0]
    lane = iota((TH, LANES), 1)

    @pl.when(left)
    def _():
        turned = pltpu.roll(sides[...], lax.rem(LANES - 16 * channel, LANES), 1)
        ts = ts_ref[0, :, 0:LANES]
        out_ref[0, :, 0:LANES] = jnp.where(lane < 8, turned + ts, out_ref[0, :, 0:LANES])

    @pl.when(right)
    def _():
        turned = pltpu.roll(sides[...], LANES - 16 - 16 * channel, 1)
        ts = ts_ref[0, :, TW - LANES : TW]
        out_ref[0, :, TW - LANES : TW] = jnp.where(
            lane >= LANES - 8, turned + ts, out_ref[0, :, TW - LANES : TW]
        )


def body(grad_x, grad_y, seam_mask, tile_offset, tables):
    CH, TH, TW = grad_x.shape
    R = lax.axis_size("row")
    C = lax.axis_size("col")
    NX, NY = TH * R, TW * C
    screen = 0.5 * math.pi * math.pi / (NX * NY)
    dims = (R, C, CH, TH, TW, screen)
    W = TW + LANES
    modes = CH * M
    crows = modes // C
    nparts = min(R, crows // 8)
    prow = crows // nparts
    ty, tx, tb, mu, cxk, cxr, cyb, cys = tables
    vmem = pl.BlockSpec(memory_space=pltpu.VMEM)
    smem = pl.BlockSpec(memory_space=pltpu.SMEM)
    anys = pl.BlockSpec(memory_space=pl.ANY)
    rows = TH + 2 * PAD
    dma = pltpu.SemaphoreType.DMA
    ts, sp = pl.pallas_call(
        functools.partial(first_kernel, dims),
        out_shape=(
            jax.ShapeDtypeStruct((CH, TH, TW), F32),
            jax.ShapeDtypeStruct((modes, M), F32),
        ),
        in_specs=[anys, anys, anys, smem, anys, anys],
        out_specs=(vmem, vmem),
        scratch_shapes=[
            pltpu.VMEM((CH, TH, TW), BF16),
            pltpu.VMEM((CH, TH, TW), BF16),
            pltpu.VMEM((TH, TW), jnp.int32),
            pltpu.VMEM((2 * CH, rows, W), F32),
            pltpu.VMEM((CH, rows, W), F32),
            pltpu.VMEM((CH, W // LANES, rows, LANES), F32),
            pltpu.VMEM((CH, W // LANES, rows, LANES), F32),
            pltpu.VMEM((rows, W), F32),
            pltpu.VMEM((TW, 4 * M), BF16),
            pltpu.VMEM((2 * M, 2 * TH), BF16),
            pltpu.VMEM((modes, M), F32),
            pltpu.VMEM((2, TH // 2, LANES), F32),
            pltpu.VMEM((2, TH // 2, LANES), F32),
            pltpu.VMEM((C, crows, M), F32),
            pltpu.VMEM((crows, M), F32),
            pltpu.VMEM((R, prow, M), F32),
            pltpu.VMEM((prow, M), F32),
            pltpu.VMEM((crows, M), F32),
            dma((3,)), dma((2,)), dma((2,)), dma((2,)), dma((4,)), dma((4,)),
            dma((C,)), dma((C,)), dma((R,)), dma((R,)),
            dma((R,)), dma((R,)), dma((C,)), dma((C,)),
        ],
        compiler_params=pltpu.CompilerParams(
            collective_id=0, has_side_effects=True, vmem_limit_bytes=58 * 2**20
        ),
        name="sums_and_sweeps",
    )(grad_x, grad_y, seam_mask, tile_offset, ty, tx)

    pos = jnp.stack([lax.axis_index("row"), lax.axis_index("col")]).astype(jnp.int32)
    spec = pltpu.PrefetchScalarGridSpec(
        num_scalar_prefetch=1,
        grid=(CH,),
        in_specs=[
            pl.BlockSpec((modes, M), lambda i, p: (0, 0)),
            pl.BlockSpec((1, TH, TW), lambda i, p: (i, 0, 0)),
            pl.BlockSpec((2, M, M), lambda i, p: (0, 0, 0)),
            pl.BlockSpec((1, M), lambda i, p: (0, 0)),
            pl.BlockSpec((M, TH + LANES), lambda i, p: (p[0], 0)),
            pl.BlockSpec((TH, 2 * M), lambda i, p: (p[0], 0)),
            pl.BlockSpec((3 * M, TW), lambda i, p: (0, p[1])),
            pl.BlockSpec((TW, M), lambda i, p: (p[1], 0)),
        ],
        out_specs=pl.BlockSpec((1, TH, TW), lambda i, p: (i, 0, 0)),
        scratch_shapes=[
            pltpu.VMEM((TH, M), F32),
            pltpu.VMEM((16 * CH, M), F32),
            pltpu.VMEM((TH, LANES), F32),
        ],
    )
    return pl.pallas_call(
        functools.partial(last_kernel, dims),
        grid_spec=spec,
        out_shape=jax.ShapeDtypeStruct((CH, TH, TW), F32),
        compiler_params=pltpu.CompilerParams(vmem_limit_bytes=58 * 2**20),
        name="synthesis",
    )(pos, sp, ts, tb, mu, cxk, cxr, cyb, cys)


def solution(mesh):
    in_specs = (
        P(None, ("groups", "row"), "col"),
        P(None, ("groups", "row"), "col"),
        P(("groups", "row"), "col"),
        P(None, "groups", None),
        P(),
    )
    out_specs = P(None, ("groups", "row"), "col")
    R, C = mesh.shape["row"], mesh.shape["col"]
    G = mesh.shape["groups"]

    def whole(grad_x, grad_y, seam_mask, tile_offset):
        NX, NY = grad_x.shape[1] // G, grad_x.shape[2]
        TH, TW = NX // R, NY // C
        W = TH + LANES
        screen = 0.5 * math.pi * math.pi / (NX * NY)
        cx, sx, ex = np_tables(NX)
        cy, sy, ey = np_tables(NY)
        ty = np.concatenate(np_split(cy) + np_split(sy), axis=1)
        tiles = [
            np.concatenate([sx[r * TH : (r + 1) * TH].T, cx[r * TH : (r + 1) * TH].T], axis=1)
            for r in range(R)
        ]
        tx = np.stack([np.concatenate(np_split(t), axis=0) for t in tiles])
        lam = ex[:, None] + ey[None, :]
        tb = np.stack([1.0 / (screen + lam), ((4.0 - lam) / (4.0 + screen)) ** SWEEPS / (screen + lam)])
        cxk = np.zeros((R, M, W))
        for r in range(R):
            cxk[r, :, :TH] = cx[r * TH : (r + 1) * TH].T
            if r > 0:
                cxk[r, :, W - 8 :] = cx[r * TH - 8 : r * TH].T
            if r < R - 1:
                cxk[r, :, TH : TH + 8] = cx[(r + 1) * TH : (r + 1) * TH + 8].T
        cxr = np.concatenate(np_split(cx), axis=1)
        hi, lo = np_split(cy.T)
        cyb = np.concatenate([hi, hi, lo], axis=0)
        tables = (
            jnp.asarray(ty), jnp.asarray(tx),
            jnp.asarray(tb.astype(np.float32)),
            jnp.asarray(ey[None, :].astype(np.float32)),
            jnp.asarray(cxk.reshape(R * M, W).astype(np.float32)),
            jnp.asarray(cxr), jnp.asarray(cyb),
            jnp.asarray(cy.astype(np.float32)),
        )
        f = jax.shard_map(body, mesh=mesh, in_specs=in_specs, out_specs=out_specs, check_vma=False)
        return f(grad_x, grad_y, seam_mask, tile_offset, tables)

    return whole
```
